256 devices in a mesh: pi: 8 (over z), pj: 4 (over x_lo, core), vert: 8 (over x_hi, y).
Axes of the slice: x: 4 (x_hi: 2, x_lo: 2; x = x_hi * 2 + x_lo), y: 4, z: 8, core: 2. Of those that a mesh axis runs over, the one named last changes fastest.
Arguments:
- amplitudes: bfloat16 [64, 64, 8, 4096], P('pi', 'pj', None, 'vert'), may hold values from -6 to 6
- ladder_ints: bfloat16 [2, 4096, 4096], P(None, 'vert'), may hold values from -0.09375 to 0.09375
- ladder_tiles: int32 [2, 2], replicated, may hold values from 0 to 7
- cycle_ints: bfloat16 [64, 5, 2, 4096], P('pj', None, None, 'vert'), may hold values from -0.3125 to 0.3125
- cycle_tiles: int32 [2, 2], replicated, may hold values from 0 to 7
- partner: int32 [8], replicated, may hold values from 0 to 7, as said below
Outputs:
- residual: float32 [64, 64, 8, 4096], P('pi', 'pj', None, 'vert')
The draws below stay inside these ranges and needn't reach their ends.
Inputs may be any that keep to these rules, and one draw needn't show every extreme that they name: `ladder_tiles`: column 0 is a residual tile, column 1 an amplitude tile, both positions in the tile list. `cycle_tiles`: column 0 is a residual tile, column 1 an amplitude tile, both positions in the tile list. partner[partner[n]] = n and partner[n] != n.
All inputs are finite; a program needn't handle non-finite values.
Results may differ from the reference program's by a relative error of at most 0.0049.
Values may be sent and summed in bfloat16 or wider, within the bound.
No kernel may reach another device: no remote copies, remote signals or barrier semaphores. Data moves between devices by JAX's collectives and lax.ppermute only.
A program may use at most 128 MiB of HBM per device.

```python
import jax
import jax.numpy as jnp
from jax import lax

TILE = 64
TILES = 8
LADDER = 2
CYCLE = 2
REACH = 2
OCC = 64
BAND = 5
TILE_SQ = 4096


def draw_partner(key, part):
    key = jax.random.fold_in(key, 7)
    order = jax.random.permutation(key, TILES).astype(jnp.int32)
    first = order[0::2]
    second = order[1::2]
    result = jnp.zeros((TILES,), jnp.int32)
    result = result.at[first].set(second)
    result = result.at[second].set(first)
    return result.astype(jnp.int32)


def set_ends(entries, own_key, low, top_value):
    index_at = [jax.random.randint(jax.random.fold_in(own_key, axis), (), 0, length) for axis, length in enumerate(entries.shape)]
    main_axis = entries.shape.index(max(entries.shape))
    beside = index_at[:main_axis] + [(index_at[main_axis] + 1) % entries.shape[main_axis]] + index_at[main_axis + 1:]
    return entries.at[tuple(index_at)].set(low).at[tuple(beside)].set(top_value)


def shard_levels(stream_key, extent, shards, low, largest):
    factor_of = 1.0
    for dim, blocks in shards:
        draws = jax.random.uniform(jax.random.fold_in(jax.random.fold_in(stream_key, 6), dim), (blocks,), jnp.float32, low / len(shards), largest / len(shards))
        factor_of = factor_of * jnp.repeat(jnp.exp(draws), extent[dim] // blocks).reshape((-1,) + (1,) * (len(extent) - 1 - dim))
    return factor_of


def normal_values(rng, dims, deviation, most, shards=(), kind=jnp.bfloat16):
    drawn = jax.random.normal(rng, dims, jnp.float32) * deviation
    if len(shards) > 0:
        drawn = shard_levels(rng, dims, shards, -0.22, 0.18) * drawn
    return jnp.clip(drawn, min=-most, max=most).astype(kind)


def setup_inputs(seed: int = 0) -> dict:
    key_list = jax.random.split(jax.random.key(seed), 7)
    return {
        "amplitudes": normal_values(key_list[0], (OCC, OCC, TILES, TILE_SQ), 1.0, 6.0, ((0, 8), (1, 4), (3, 8))),
        "ladder_ints": normal_values(key_list[1], (LADDER, TILE_SQ, TILE_SQ), TILE_SQ ** -0.5, 0.09375, ((1, 8),)),
        "ladder_tiles": set_ends(jax.random.randint(key_list[2], (LADDER, 2), 0, TILES), jax.random.fold_in(key_list[2], 1), 0, TILES - 1).astype(jnp.int32),
        "cycle_ints": normal_values(key_list[3], (OCC, BAND, CYCLE, TILE_SQ), (BAND * TILE) ** -0.5, 0.3125, ((0, 4), (3, 8))),
        "cycle_tiles": set_ends(jax.random.randint(key_list[4], (CYCLE, 2), 0, TILES), jax.random.fold_in(key_list[4], 1), 0, TILES - 1).astype(jnp.int32),
        "partner": draw_partner(jax.random.fold_in(key_list[6], 71), 0),
    }


def reference(amplitudes, ladder_ints, ladder_tiles, cycle_ints, cycle_tiles, partner):
    tile_ids = jnp.arange(TILES, dtype=jnp.int32)
    total = jnp.zeros((OCC, OCC, TILES, TILE_SQ), jnp.float32)
    for which in range(LADDER):
        source = lax.dynamic_index_in_dim(amplitudes, ladder_tiles[which, 1].astype(jnp.int32), 2, keepdims=False)
        product = jnp.dot(source.reshape(OCC * OCC, TILE_SQ), ladder_ints[which].T, preferred_element_type=jnp.float32)
        selector = (tile_ids == ladder_tiles[which, 0].astype(jnp.int32)).astype(jnp.float32)
        total = total + selector[None, None, :, None] * product.reshape(OCC, OCC, 1, TILE_SQ)
    padded = jnp.pad(amplitudes, ((0, 0), (REACH, REACH), (0, 0), (0, 0)))
    for which in range(CYCLE):
        source = lax.dynamic_index_in_dim(padded, cycle_tiles[which, 1].astype(jnp.int32), 2, keepdims=False)
        source = source.reshape(OCC, OCC + 2 * REACH, TILE, TILE).astype(jnp.float32)
        cycle = jnp.zeros((OCC, OCC, TILE, TILE), jnp.float32)
        for offset in range(BAND):
            kernel = cycle_ints[:, offset, which].reshape(OCC, TILE, TILE).astype(jnp.float32)
            cycle = cycle + jnp.einsum("ijac,jcb->ijab", source[:, offset:offset + OCC], kernel)
        selector = (tile_ids == cycle_tiles[which, 0].astype(jnp.int32)).astype(jnp.float32)
        total = total + selector[None, None, :, None] * cycle.reshape(OCC, OCC, 1, TILE_SQ)
    raw = total.astype(jnp.bfloat16)
    mirrored = jnp.take(raw, partner.astype(jnp.int32), axis=2).reshape(OCC, OCC, TILES, TILE, TILE)
    mirrored = jnp.transpose(mirrored, (1, 0, 2, 4, 3)).reshape(OCC, OCC, TILES, TILE_SQ)
    return raw.astype(jnp.float32) + mirrored.astype(jnp.float32)
```

```python
import jax
import jax.numpy as jnp
import numpy as np
from jax import lax
from jax.experimental import pallas as pl
from jax.experimental.pallas import tpu as pltpu
from jax.sharding import PartitionSpec as P

TILE = 64
REACH = 2
BAND = 5
ROWS = 8
LANES = 512
PAIRS = 128
BF = jnp.bfloat16
F32 = jnp.float32
MIB = 1 << 20


def vert_moves(move):
    return [(v, move(v // 4, v % 4)) for v in range(8)]


FLIP = vert_moves(lambda h, y: (1 - h) * 4 + y)
UP = vert_moves(lambda h, y: h * 4 + (y + 1) % 4)
DOWN = vert_moves(lambda h, y: h * 4 + (y + 3) % 4)


def pair_moves(k):
    return [
        (p * 4 + q, (2 * q + ((p % 2) ^ k)) * 4 + p // 2) for p in range(8) for q in range(4)
    ]


def send_order():
    row = np.arange(1024)
    slot, a, v, b = row // 512, (row // 64) % 8, (row // 8) % 8, row % 8
    return v * 128 + slot * 64 + b * 8 + a


def place_order():
    row = np.arange(1024)
    v, slot, b, a = row // 128, (row // 64) % 2, (row // 8) % 8, row % 8
    return slot * 512 + b * 64 + v * 8 + a


def permutation(order):
    columns = lax.broadcasted_iota(jnp.int32, (1024, 1024), 1)
    return (jnp.asarray(order, jnp.int32)[:, None] == columns).astype(BF)


def pack_outgoing(total, swap, parity, first_ref, second_ref):
    sent = jnp.dot(total.astype(BF), swap, preferred_element_type=F32).astype(BF)
    low, high = sent[:64], sent[64:]
    first = jnp.where(parity == 0, low, high)
    second = jnp.where(parity == 0, high, low)
    for v in range(8):
        first_ref[v] = first[:, v * 128 : (v + 1) * 128]
        second_ref[v] = second[:, v * 128 : (v + 1) * 128]


def ladder_kernel(scalars, ints, swap, *refs):
    pieces, (total_ref, first_ref, second_ref) = refs[:8], refs[8:]
    sums = []
    for which in range(2):
        acc = None
        for d in range(8):
            start = pl.multiple_of(scalars[1 + d] * LANES, LANES)
            part = lax.dot_general(
                pieces[d][which * PAIRS : (which + 1) * PAIRS, :],
                ints[which, :, pl.ds(start, LANES)],
                (((1,), (1,)), ((), ())),
                preferred_element_type=F32,
            )
            acc = part if acc is None else acc + part
        sums.append(acc)
    total = jnp.concatenate(sums, axis=1)
    total_ref[...] = total
    pack_outgoing(total, swap[...], scalars[0], first_ref, second_ref)


def cycle_kernel(scalars, before, inner, after, swap, *refs):
    pieces, (total_ref, first_ref, second_ref, ints) = refs[:8], refs[8:]
    for d in range(8):
        ints[scalars[1 + d]] = pieces[d][256:, :].astype(F32)

    def rows_of(j):
        if j < REACH:
            return before[j]
        if j < REACH + 16:
            return inner[j - REACH]
        return after[j - REACH - 16]

    laid = []
    for j in range(16 + 2 * REACH):
        block = rows_of(j)
        laid.append(
            jnp.concatenate([block[:, a * TILE : (a + 1) * TILE] for a in range(ROWS)], axis=0)
        )
    lane = lax.broadcasted_iota(jnp.int32, (8, 128), 1)
    low = lane < TILE
    for j in range(16):
        left = jnp.concatenate([laid[j + o] for o in range(BAND)], axis=1)
        right = jnp.concatenate(
            [
                ints[v, (j // 4) * 40 + o * 8 : (j // 4) * 40 + o * 8 + 8, (j % 4) * 128 : (j % 4) * 128 + 128]
                for o in range(BAND)
                for v in range(8)
            ],
            axis=0,
        ).astype(BF)
        done = jnp.dot(left, right, preferred_element_type=F32)
        for r in range(2):
            for t in range(4):
                even = done[t * 32 + r * 8 : t * 32 + r * 8 + 8]
                odd = done[t * 32 + 16 + r * 8 : t * 32 + 16 + r * 8 + 8]
                if r == 0:
                    odd = pltpu.roll(odd, TILE, 1)
                else:
                    even = pltpu.roll(even, TILE, 1)
                total_ref[j * 8 : j * 8 + 8, r * LANES + t * 128 : r * LANES + (t + 1) * 128] = (
                    jnp.where(low, even, odd)
                )
    pack_outgoing(total_ref[...], swap[...], scalars[0], first_ref, second_ref)


def finish_kernel(scalars, ladder, cycle, arrived, place, out_ref, mirrored):
    parity = scalars[0]
    wide = jnp.concatenate([arrived[v] for v in range(8)], axis=1)
    moved = jnp.dot(wide, place[...], preferred_element_type=F32)
    for k in range(2):
        half = parity ^ k
        mirrored[0, half] = moved[k * 64 : k * 64 + 64]
        mirrored[1, half] = moved[128 + k * 64 : 128 + k * 64 + 64]
    tile = lax.broadcasted_iota(jnp.int32, (8, LANES), 0)
    own = [(tile == scalars[9 + s]).astype(F32) for s in range(4)]
    other = [(tile == scalars[13 + s]).astype(F32) for s in range(4)]

    def one(i):
        for j in range(16):
            row = j * 8 + i
            mrow = i * 8 + j % 8
            acc = None
            for s in range(4):
                source = ladder if s < 2 else cycle
                lanes = slice((s % 2) * LANES, (s % 2 + 1) * LANES)
                term = own[s] * source[pl.ds(row, 1), lanes]
                acc = term if acc is None else acc + term
                acc = acc + other[s] * mirrored[s // 2, j // 8, pl.ds(mrow, 1), lanes]
            out_ref[i, j] = acc

    pl.loop(0, 8)(one)


def call(kernel, outs, scratch=(), limit=24, flops=0, moved=0):
    def run(scalars, *args):
        return pl.pallas_call(
            kernel,
            out_shape=outs,
            in_specs=[pl.BlockSpec(memory_space=pltpu.SMEM)]
            + [pl.BlockSpec(memory_space=pltpu.VMEM)] * len(args),
            out_specs=jax.tree.map(lambda _: pl.BlockSpec(memory_space=pltpu.VMEM), outs),
            scratch_shapes=list(scratch),
            compiler_params=pltpu.CompilerParams(vmem_limit_bytes=limit * MIB),
            cost_estimate=pl.CostEstimate(flops=flops, bytes_accessed=moved, transcendentals=0),
        )(scalars, *args)

    return run


def select(amplitudes, index):
    tile = lax.dynamic_index_in_dim(amplitudes, index, 2, keepdims=False)
    return jnp.transpose(tile, (1, 0, 2))


def body(amplitudes, ladder_ints, ladder_tiles, cycle_ints, cycle_tiles, partner):
    pi, vert = lax.axis_index("pi"), lax.axis_index("vert")
    h, y = vert // 4, vert % 4
    sources = [
        (h, y), (1 - h, y), (h, y + 3), (h, y + 1),
        (1 - h, y + 3), (1 - h, y + 1), (h, y + 2), (1 - h, y + 2),
    ]
    dests = jnp.concatenate([ladder_tiles[:, 0], cycle_tiles[:, 0]])
    scalars = jnp.concatenate(
        [
            jnp.stack([pi % 2] + [a * 4 + b % 4 for a, b in sources]).astype(jnp.int32),
            dests,
            partner[dests],
        ]
    )
    cycle_in = jnp.stack([select(amplitudes, cycle_tiles[r, 1]) for r in range(2)], axis=1)
    cycle_in = cycle_in.reshape(16, 16, LANES)
    up = [(q, q + 1) for q in range(3)]
    down = [(q + 1, q) for q in range(3)]
    before = lax.ppermute(cycle_in[-REACH:], "pj", up)
    after = lax.ppermute(cycle_in[:REACH], "pj", down)

    ladder_in = jnp.stack([select(amplitudes, ladder_tiles[w, 1]) for w in range(2)])
    ints = cycle_ints.reshape(4, 4, BAND, 2, ROWS, TILE)
    ints = jnp.transpose(ints, (0, 2, 4, 1, 3, 5)).reshape(160, LANES)
    own = jnp.concatenate([ladder_in.reshape(256, LANES), ints])
    flip = lax.ppermute(own, "vert", FLIP)
    own_up = lax.ppermute(own, "vert", UP)
    own_down = lax.ppermute(own, "vert", DOWN)
    flip_up = lax.ppermute(flip, "vert", UP)
    flip_down = lax.ppermute(flip, "vert", DOWN)
    far = lax.ppermute(own_up, "vert", UP)
    flip_far = lax.ppermute(flip_down, "vert", DOWN)
    pieces = [own, flip, own_up, own_down, flip_up, flip_down, far, flip_far]

    swap = permutation(send_order())
    packed = [jax.ShapeDtypeStruct((8, 64, 128), BF)] * 2
    outs = [jax.ShapeDtypeStruct((PAIRS, 1024), F32)] + packed
    ladder, ladder_0, ladder_1 = call(ladder_kernel, outs)(scalars, ladder_ints, swap, *pieces)
    cycle, cycle_0, cycle_1 = call(
        cycle_kernel, outs, [pltpu.VMEM((8, 160, LANES), F32)]
    )(scalars, before, cycle_in, after, swap, *pieces)

    sent = [
        lax.ppermute(block, ("pi", "pj"), pair_moves(k))
        for k, block in ((0, ladder_0), (1, ladder_1), (0, cycle_0), (1, cycle_1))
    ]
    arrived = lax.all_to_all(jnp.concatenate(sent, axis=1), "vert", 0, 0)
    return call(
        finish_kernel,
        jax.ShapeDtypeStruct((8, 16, 8, LANES), F32),
        [pltpu.VMEM((2, 2, 64, 1024), F32)],
    )(scalars, ladder, cycle, arrived, permutation(place_order()))


def solution(mesh):
    placed = (
        P("pi", "pj", None, "vert"),
        P(None, "vert", None),
        P(),
        P("pj", None, None, "vert"),
        P(),
        P(),
    )
    return jax.shard_map(
        body, mesh=mesh, in_specs=placed, out_specs=P("pi", "pj", None, "vert"), check_vma=False
    )
```

```python
import jax
import jax.numpy as jnp
import numpy as np
from jax import lax
from jax.experimental import pallas as pl
from jax.experimental.pallas import tpu as pltpu
from jax.sharding import PartitionSpec as P

TILE = 64
REACH = 2
BAND = 5
ROWS = 8
LANES = 512
PAIRS = 128
BF = jnp.bfloat16
F32 = jnp.float32
MIB = 1 << 20


def vert_moves(move):
    return [(v, move(v // 4, v % 4)) for v in range(8)]


FLIP = vert_moves(lambda h, y: (1 - h) * 4 + y)
UP = vert_moves(lambda h, y: h * 4 + (y + 1) % 4)
DOWN = vert_moves(lambda h, y: h * 4 + (y + 3) % 4)


def pair_moves(k):
    return [
        (p * 4 + q, (2 * q + ((p % 2) ^ k)) * 4 + p // 2) for p in range(8) for q in range(4)
    ]


def send_order():
    row = np.arange(1024)
    slot, a, v, b = row // 512, (row // 64) % 8, (row // 8) % 8, row % 8
    return v * 128 + slot * 64 + b * 8 + a


def place_order():
    row = np.arange(1024)
    v, slot, b, a = row // 128, (row // 64) % 2, (row // 8) % 8, row % 8
    return slot * 512 + b * 64 + v * 8 + a


def permutation(order):
    columns = lax.broadcasted_iota(jnp.int32, (1024, 1024), 1)
    return (jnp.asarray(order, jnp.int32)[:, None] == columns).astype(BF)


def prepare_kernel(ladder_tiles, cycle_tiles, amplitudes, ints, own_ref, inner_ref, first_ref, last_ref, wide, tall):
    row = lax.broadcasted_iota(jnp.int32, (512, 128), 0)
    column = lax.broadcasted_iota(jnp.int32, (512, 128), 1)
    ladder_row = row < 256
    i = row & 7
    j = jnp.where(ladder_row, (row >> 3) & 15, (row >> 4) & 15)
    which = jnp.where(ladder_row, (row >> 7) & 1, (row >> 3) & 1)
    ladder_0, cycle_0 = ladder_tiles[0, 1], cycle_tiles[0, 1]
    tile = jnp.where(
        ladder_row,
        ladder_0 + which * (ladder_tiles[1, 1] - ladder_0),
        cycle_0 + which * (cycle_tiles[1, 1] - cycle_0),
    )
    wanted = (i * 16 + j) * 8 + tile - column
    pick = jnp.concatenate(
        [jnp.where(wanted == c * 128, 1.0, 0.0).astype(BF) for c in range(8)], axis=1
    )
    picked = jnp.dot(pick, amplitudes[...], preferred_element_type=F32).astype(BF)
    own_ref[:256, :] = picked[:256]
    inner = picked[256:].reshape(16, 16, LANES)
    inner_ref[...] = inner
    first_ref[...] = inner[:REACH]
    last_ref[...] = inner[16 - REACH :]
    for t in range(4):
        wide[t] = ints[:, t * 128 : (t + 1) * 128].astype(F32)
    low = lax.broadcasted_iota(jnp.int32, (80, 128), 1) < TILE
    for t in range(4):
        zero = wide[t, pl.ds(0, 80, stride=2), :]
        one = wide[t, pl.ds(1, 80, stride=2), :]
        tall[pl.ds(2 * t, 80, stride=8), :] = jnp.where(low, zero, pltpu.roll(one, TILE, 1))
        tall[pl.ds(2 * t + 1, 80, stride=8), :] = jnp.where(low, pltpu.roll(zero, TILE, 1), one)
    for b in range(4):
        own_ref[256:, b * 128 : (b + 1) * 128] = tall[b * 160 : (b + 1) * 160, :].astype(BF)


def source_rows():
    vert = lax.axis_index("vert")
    h, y = vert // 4, vert % 4
    places = [
        (h, y), (1 - h, y), (h, y + 3), (h, y + 1),
        (1 - h, y + 3), (1 - h, y + 1), (h, y + 2), (1 - h, y + 2),
    ]
    return [a * 4 + b % 4 for a, b in places]


def main_kernel(ladder_hbm, before, inner, after, swap, *refs):
    pieces, (total_ref, sent_ref, ladder_ints, ints, total, sem, sems) = refs[:8], refs[8:]
    loads = [
        pltpu.make_async_copy(ladder_hbm.at[w], ladder_ints.at[w], sems.at[w]) for w in range(2)
    ]
    for load in loads:
        load.start()
    sources = source_rows()
    parity = lax.axis_index("pi") % 2
    for d in range(8):
        ints[sources[d]] = pieces[d][256:, :].astype(F32)

    def rows_of(j):
        if j < REACH:
            return before[j]
        if j < REACH + 16:
            return inner[j - REACH]
        return after[j - REACH - 16]

    laid = []
    for j in range(16 + 2 * REACH):
        block = rows_of(j)
        laid.append(
            jnp.concatenate([block[:, a * TILE : (a + 1) * TILE] for a in range(ROWS)], axis=0)
        )
    low = lax.broadcasted_iota(jnp.int32, (8, 128), 1) < TILE
    for j in range(16):
        left = jnp.concatenate([laid[j + o] for o in range(BAND)], axis=1)
        base, lanes = (j % 4) * 40, (j // 4) * 128
        right = jnp.concatenate(
            [
                ints[v, base + o * 8 : base + o * 8 + 8, lanes : lanes + 128]
                for o in range(BAND)
                for v in range(8)
            ],
            axis=0,
        ).astype(BF)
        done = jnp.dot(left, right, preferred_element_type=F32)
        for r in range(2):
            for t in range(4):
                even = done[t * 32 + r * 8 : t * 32 + r * 8 + 8]
                odd = done[t * 32 + 16 + r * 8 : t * 32 + 16 + r * 8 + 8]
                if r == 0:
                    odd = pltpu.roll(odd, TILE, 1)
                else:
                    even = pltpu.roll(even, TILE, 1)
                lane = 1024 + r * LANES + t * 128
                total[j * 8 : j * 8 + 8, lane : lane + 128] = jnp.where(low, even, odd)
    for which in range(2):
        loads[which].wait()
        acc = None
        for d in range(8):
            start = pl.multiple_of(sources[d] * LANES, LANES)
            part = lax.dot_general(
                pieces[d][which * PAIRS : (which + 1) * PAIRS, :],
                ladder_ints[which, :, pl.ds(start, LANES)],
                (((1,), (1,)), ((), ())),
                preferred_element_type=F32,
            )
            acc = part if acc is None else acc + part
        total[:, which * LANES : (which + 1) * LANES] = acc
    keep = pltpu.make_async_copy(total, total_ref, sem)
    keep.start()
    for s in range(2):
        sent = jnp.dot(
            total[:, s * 1024 : (s + 1) * 1024].astype(BF), swap[...], preferred_element_type=F32
        ).astype(BF)
        upper, under = sent[:64], sent[64:]
        halves = (
            jnp.where(parity == 0, upper, under),
            jnp.where(parity == 0, under, upper),
        )
        for k in range(2):
            for v in range(8):
                sent_ref[v, k, s * 64 : (s + 1) * 64, :] = halves[k][:, v * 128 : (v + 1) * 128]
    keep.wait()


def finish_kernel(ladder_tiles, cycle_tiles, partner, total_ref, first, second, place, out_ref, mirrored, total, sem):
    fetch = pltpu.make_async_copy(total_ref, total, sem)
    fetch.start()
    parity = lax.axis_index("pi") % 2
    for k, arrived in enumerate((first, second)):
        wide = jnp.concatenate([arrived[v] for v in range(8)], axis=1)
        moved = jnp.dot(wide, place[...], preferred_element_type=F32)
        for s in range(2):
            mirrored[s, parity ^ k] = moved[s * 64 : (s + 1) * 64]
    dests = [ladder_tiles[0, 0], ladder_tiles[1, 0], cycle_tiles[0, 0], cycle_tiles[1, 0]]
    tile = lax.broadcasted_iota(jnp.int32, (8, LANES), 0)
    own = [(tile == dest).astype(F32) for dest in dests]
    other = [(tile == partner[dest]).astype(F32) for dest in dests]
    fetch.wait()

    def one(i):
        for j in range(16):
            acc = None
            for s in range(4):
                lanes = slice((s % 2) * LANES, (s % 2 + 1) * LANES)
                term = own[s] * total[pl.ds(j * 8 + i, 1), s * LANES : (s + 1) * LANES]
                acc = term if acc is None else acc + term
                acc = acc + other[s] * mirrored[s // 2, j // 8, pl.ds(i * 8 + j % 8, 1), lanes]
            out_ref[i, j] = acc

    pl.loop(0, 8)(one)


SMEM = pl.BlockSpec(memory_space=pltpu.SMEM)
VMEM = pl.BlockSpec(memory_space=pltpu.VMEM)
ANY = pl.BlockSpec(memory_space=pl.ANY)


def call(kernel, ins, outs, out_specs, scratch, limit, flops):
    return pl.pallas_call(
        kernel,
        out_shape=outs,
        in_specs=ins,
        out_specs=out_specs,
        scratch_shapes=scratch,
        compiler_params=pltpu.CompilerParams(vmem_limit_bytes=limit * MIB),
        cost_estimate=pl.CostEstimate(flops=flops, bytes_accessed=4 * MIB, transcendentals=0),
    )


def shape(dims, kind):
    return jax.ShapeDtypeStruct(dims, kind)


def body(amplitudes, ladder_ints, ladder_tiles, cycle_ints, cycle_tiles, partner):
    edge = shape((REACH, 16, LANES), BF)
    own, inner, first, last = call(
        prepare_kernel,
        [SMEM, SMEM, VMEM, VMEM],
        [shape((416, LANES), BF), shape((16, 16, LANES), BF), edge, edge],
        [VMEM] * 4,
        [pltpu.VMEM((4, 160, 128), F32), pltpu.VMEM((640, 128), F32)],
        12,
        10**9,
    )(ladder_tiles, cycle_tiles, amplitudes.reshape(1024, LANES), cycle_ints.reshape(160, LANES))
    flip = lax.ppermute(own, "vert", FLIP)
    own_up = lax.ppermute(own, "vert", UP)
    own_down = lax.ppermute(own, "vert", DOWN)
    flip_up = lax.ppermute(flip, "vert", UP)
    flip_down = lax.ppermute(flip, "vert", DOWN)
    far = lax.ppermute(own_up, "vert", UP)
    flip_far = lax.ppermute(flip_down, "vert", DOWN)
    before = lax.ppermute(last, "pj", [(q, q + 1) for q in range(3)])
    after = lax.ppermute(first, "pj", [(q + 1, q) for q in range(3)])
    pieces = [own, flip, own_up, own_down, flip_up, flip_down, far, flip_far]

    total, sent = call(
        main_kernel,
        [ANY] + [VMEM] * 12,
        [shape((PAIRS, 2048), F32), shape((8, 2, 128, 128), BF)],
        [ANY, VMEM],
        [
            pltpu.VMEM((2, LANES, 4096), BF),
            pltpu.VMEM((8, 160, LANES), F32),
            pltpu.VMEM((PAIRS, 2048), F32),
            pltpu.SemaphoreType.DMA,
            pltpu.SemaphoreType.DMA((2,)),
        ],
        26,
        2 * 10**9,
    )(ladder_ints, before, inner, after, permutation(send_order()), *pieces)
    arrived = lax.all_to_all(sent, "vert", 0, 0)
    moved = [lax.ppermute(arrived[:, k], ("pi", "pj"), pair_moves(k)) for k in range(2)]
    return call(
        finish_kernel,
        [SMEM, SMEM, SMEM, ANY, VMEM, VMEM, VMEM],
        shape((8, 16, 8, LANES), F32),
        VMEM,
        [
            pltpu.VMEM((2, 2, 64, 1024), F32),
            pltpu.VMEM((PAIRS, 2048), F32),
            pltpu.SemaphoreType.DMA,
        ],
        16,
        10**9,
    )(ladder_tiles, cycle_tiles, partner, total, *moved, permutation(place_order()))


def solution(mesh):
    placed = (
        P("pi", "pj", None, "vert"),
        P(None, "vert", None),
        P(),
        P("pj", None, None, "vert"),
        P(),
        P(),
    )
    return jax.shard_map(
        body, mesh=mesh, in_specs=placed, out_specs=P("pi", "pj", None, "vert"), check_vma=False
    )
```

```python
import jax
import jax.numpy as jnp
import numpy as np
from jax import lax
from jax.experimental import pallas as pl
from jax.experimental.pallas import tpu as pltpu
from jax.sharding import PartitionSpec as P

TILE = 64
REACH = 2
BAND = 5
ROWS = 8
LANES = 512
PAIRS = 128
BF = jnp.bfloat16
F32 = jnp.float32
MIB = 1 << 20


def vert_moves(move):
    return [(v, move(v // 4, v % 4)) for v in range(8)]


FLIP = vert_moves(lambda h, y: (1 - h) * 4 + y)
UP = vert_moves(lambda h, y: h * 4 + (y + 1) % 4)
DOWN = vert_moves(lambda h, y: h * 4 + (y + 3) % 4)


def pair_moves(k):
    return [
        (p * 4 + q, (2 * q + ((p % 2) ^ k)) * 4 + p // 2) for p in range(8) for q in range(4)
    ]


def send_order():
    row = np.arange(1024)
    slot, a, v, b = row // 512, (row // 64) % 8, (row // 8) % 8, row % 8
    return v * 128 + slot * 64 + b * 8 + a


def place_order():
    row = np.arange(1024)
    v, slot, b, a = row // 128, (row // 64) % 2, (row // 8) % 8, row % 8
    return slot * 512 + b * 64 + v * 8 + a


def permutation(order):
    columns = lax.broadcasted_iota(jnp.int32, (1024, 1024), 1)
    return (jnp.asarray(order, jnp.int32)[:, None] == columns).astype(BF)


def prepare_kernel(ladder_tiles, cycle_tiles, amplitudes, ints, ladder_ref, ints_ref, inner_ref, first_ref, last_ref, wide, tall):
    row = lax.broadcasted_iota(jnp.int32, (512, 128), 0)
    column = lax.broadcasted_iota(jnp.int32, (512, 128), 1)
    ladder_row = row < 256
    i = row & 7
    j = jnp.where(ladder_row, (row >> 3) & 15, (row >> 4) & 15)
    which = jnp.where(ladder_row, (row >> 7) & 1, (row >> 3) & 1)
    ladder_0, cycle_0 = ladder_tiles[0, 1], cycle_tiles[0, 1]
    tile = jnp.where(
        ladder_row,
        ladder_0 + which * (ladder_tiles[1, 1] - ladder_0),
        cycle_0 + which * (cycle_tiles[1, 1] - cycle_0),
    )
    wanted = (i * 16 + j) * 8 + tile - column
    pick = jnp.concatenate(
        [jnp.where(wanted == c * 128, 1.0, 0.0).astype(BF) for c in range(8)], axis=1
    )
    picked = jnp.dot(pick, amplitudes[...], preferred_element_type=F32).astype(BF)
    ladder_ref[...] = picked[:256]
    inner = picked[256:].reshape(16, 16, LANES)
    inner_ref[...] = inner
    first_ref[...] = inner[:REACH]
    last_ref[...] = inner[16 - REACH :]
    for t in range(4):
        wide[t] = ints[:, t * 128 : (t + 1) * 128].astype(F32)
    low = lax.broadcasted_iota(jnp.int32, (80, 128), 1) < TILE
    for t in range(4):
        zero = wide[t, pl.ds(0, 80, stride=2), :]
        one = wide[t, pl.ds(1, 80, stride=2), :]
        tall[pl.ds(2 * t, 80, stride=8), :] = jnp.where(low, zero, pltpu.roll(one, TILE, 1))
        tall[pl.ds(2 * t + 1, 80, stride=8), :] = jnp.where(low, pltpu.roll(zero, TILE, 1), one)
    for b in range(4):
        ints_ref[:, b * 128 : (b + 1) * 128] = tall[b * 160 : (b + 1) * 160, :].astype(BF)


def split_pieces(refs, rows):
    own, flip, up, down, far, flip_far = refs
    vert = lax.axis_index("vert")
    h, y = vert // 4, vert % 4
    first, second = pl.ds(0, rows), pl.ds(rows, rows)
    pieces = [
        (h, y, own, first), (1 - h, y, flip, first),
        (h, y + 3, up, first), (1 - h, y + 3, up, second),
        (h, y + 1, down, first), (1 - h, y + 1, down, second),
        (h, y + 2, far, first), (1 - h, y + 2, flip_far, first),
    ]
    return [(a * 4 + b % 4, ref, where) for a, b, ref, where in pieces]


def pack(total, swap, sent_ref):
    parity = lax.axis_index("pi") % 2
    sent = jnp.dot(total[...].astype(BF), swap[...], preferred_element_type=F32).astype(BF)
    upper, under = sent[:64], sent[64:]
    halves = (jnp.where(parity == 0, upper, under), jnp.where(parity == 0, under, upper))
    for k in range(2):
        for v in range(8):
            sent_ref[v, k] = halves[k][:, v * 128 : (v + 1) * 128]


def ladder_kernel(ladder_hbm, swap, *refs):
    total_ref, sent_ref, ladder_ints, total, sem, sems = refs[6:]
    loads = [
        pltpu.make_async_copy(ladder_hbm.at[w], ladder_ints.at[w], sems.at[w]) for w in range(2)
    ]
    for load in loads:
        load.start()
    pieces = split_pieces(refs[:6], 256)
    for which in range(2):
        loads[which].wait()
        acc = None
        for source, ref, where in pieces:
            start = pl.multiple_of(source * LANES, LANES)
            part = lax.dot_general(
                ref[pl.ds(where.start + which * PAIRS, PAIRS), :],
                ladder_ints[which, :, pl.ds(start, LANES)],
                (((1,), (1,)), ((), ())),
                preferred_element_type=F32,
            )
            acc = part if acc is None else acc + part
        total[:, which * LANES : (which + 1) * LANES] = acc
    keep = pltpu.make_async_copy(total, total_ref, sem)
    keep.start()
    pack(total, swap, sent_ref)
    keep.wait()


def cycle_kernel(before, inner, after, swap, *refs):
    total_ref, sent_ref, ints, total, sem = refs[6:]
    for source, ref, where in split_pieces(refs[:6], 160):
        ints[source] = ref[where, :].astype(F32)

    def rows_of(j):
        if j < REACH:
            return before[j]
        if j < REACH + 16:
            return inner[j - REACH]
        return after[j - REACH - 16]

    laid = []
    for j in range(16 + 2 * REACH):
        block = rows_of(j)
        laid.append(
            jnp.concatenate([block[:, a * TILE : (a + 1) * TILE] for a in range(ROWS)], axis=0)
        )
    low = lax.broadcasted_iota(jnp.int32, (8, 128), 1) < TILE
    for j in range(16):
        left = jnp.concatenate([laid[j + o] for o in range(BAND)], axis=1)
        base, lanes = (j % 4) * 40, (j // 4) * 128
        right = jnp.concatenate(
            [
                ints[v, base + o * 8 : base + o * 8 + 8, lanes : lanes + 128]
                for o in range(BAND)
                for v in range(8)
            ],
            axis=0,
        ).astype(BF)
        done = jnp.dot(left, right, preferred_element_type=F32)
        for r in range(2):
            for t in range(4):
                even = done[t * 32 + r * 8 : t * 32 + r * 8 + 8]
                odd = done[t * 32 + 16 + r * 8 : t * 32 + 16 + r * 8 + 8]
                if r == 0:
                    odd = pltpu.roll(odd, TILE, 1)
                else:
                    even = pltpu.roll(even, TILE, 1)
                lane = r * LANES + t * 128
                total[j * 8 : j * 8 + 8, lane : lane + 128] = jnp.where(low, even, odd)
    keep = pltpu.make_async_copy(total, total_ref, sem)
    keep.start()
    pack(total, swap, sent_ref)
    keep.wait()


def finish_kernel(ladder_tiles, cycle_tiles, partner, ladder_total, cycle_total, place, *refs):
    arrived, (out_ref, mirrored, total, sems) = refs[:4], refs[4:]
    fetches = [
        pltpu.make_async_copy(source, total.at[s], sems.at[s])
        for s, source in enumerate((ladder_total, cycle_total))
    ]
    for fetch in fetches:
        fetch.start()
    parity = lax.axis_index("pi") % 2
    for s in range(2):
        for k in range(2):
            block = arrived[s * 2 + k]
            wide = jnp.concatenate([block[v] for v in range(8)], axis=1)
            mirrored[s, parity ^ k] = jnp.dot(wide, place[...], preferred_element_type=F32)
    dests = [ladder_tiles[0, 0], ladder_tiles[1, 0], cycle_tiles[0, 0], cycle_tiles[1, 0]]
    tile = lax.broadcasted_iota(jnp.int32, (8, LANES), 0)
    own = [(tile == dest).astype(F32) for dest in dests]
    other = [(tile == partner[dest]).astype(F32) for dest in dests]
    for fetch in fetches:
        fetch.wait()

    def one(i):
        for j in range(16):
            acc = None
            for s in range(4):
                lanes = slice((s % 2) * LANES, (s % 2 + 1) * LANES)
                term = own[s] * total[s // 2, pl.ds(j * 8 + i, 1), lanes]
                acc = term if acc is None else acc + term
                acc = acc + other[s] * mirrored[s // 2, j // 8, pl.ds(i * 8 + j % 8, 1), lanes]
            out_ref[i, j] = acc

    pl.loop(0, 8)(one)


SMEM = pl.BlockSpec(memory_space=pltpu.SMEM)
VMEM = pl.BlockSpec(memory_space=pltpu.VMEM)
ANY = pl.BlockSpec(memory_space=pl.ANY)


def call(kernel, ins, outs, out_specs, scratch, limit, flops):
    return pl.pallas_call(
        kernel,
        out_shape=outs,
        in_specs=ins,
        out_specs=out_specs,
        scratch_shapes=scratch,
        compiler_params=pltpu.CompilerParams(vmem_limit_bytes=limit * MIB),
        cost_estimate=pl.CostEstimate(flops=flops, bytes_accessed=4 * MIB, transcendentals=0),
    )


def shape(dims, kind):
    return jax.ShapeDtypeStruct(dims, kind)


def gather(own):
    rows = own.shape[0]
    flip = lax.ppermute(own, "vert", FLIP)
    both = jnp.concatenate([own, flip])
    up = lax.ppermute(both, "vert", UP)
    down = lax.ppermute(both, "vert", DOWN)
    far = lax.ppermute(up[:rows], "vert", UP)
    flip_far = lax.ppermute(down[rows:], "vert", DOWN)
    return [own, flip, up, down, far, flip_far]


def exchange(sent):
    arrived = lax.all_to_all(sent, "vert", 0, 0)
    return [lax.ppermute(arrived[:, k], ("pi", "pj"), pair_moves(k)) for k in range(2)]


def body(amplitudes, ladder_ints, ladder_tiles, cycle_ints, cycle_tiles, partner):
    edge = shape((REACH, 16, LANES), BF)
    ladder_own, ints_own, inner, first, last = call(
        prepare_kernel,
        [SMEM, SMEM, VMEM, VMEM],
        [shape((256, LANES), BF), shape((160, LANES), BF), shape((16, 16, LANES), BF), edge, edge],
        [VMEM] * 5,
        [pltpu.VMEM((4, 160, 128), F32), pltpu.VMEM((640, 128), F32)],
        12,
        10**9,
    )(ladder_tiles, cycle_tiles, amplitudes.reshape(1024, LANES), cycle_ints.reshape(160, LANES))
    swap, place = permutation(send_order()), permutation(place_order())
    outs = [shape((PAIRS, 1024), F32), shape((8, 2, 64, 128), BF)]

    ints_pieces = gather(ints_own)
    before = lax.ppermute(last, "pj", [(q, q + 1) for q in range(3)])
    after = lax.ppermute(first, "pj", [(q + 1, q) for q in range(3)])
    cycle_total, cycle_sent = call(
        cycle_kernel,
        [VMEM] * 10,
        outs,
        [ANY, VMEM],
        [
            pltpu.VMEM((8, 160, LANES), F32),
            pltpu.VMEM((PAIRS, 1024), F32),
            pltpu.SemaphoreType.DMA,
        ],
        16,
        10**9,
    )(before, inner, after, swap, *ints_pieces)
    cycle_moved = exchange(cycle_sent)

    ladder_pieces = gather(ladder_own)
    ladder_total, ladder_sent = call(
        ladder_kernel,
        [ANY] + [VMEM] * 7,
        outs,
        [ANY, VMEM],
        [
            pltpu.VMEM((2, LANES, 4096), BF),
            pltpu.VMEM((PAIRS, 1024), F32),
            pltpu.SemaphoreType.DMA,
            pltpu.SemaphoreType.DMA((2,)),
        ],
        50,
        2 * 10**9,
    )(ladder_ints, swap, *ladder_pieces)
    ladder_moved = exchange(ladder_sent)

    return call(
        finish_kernel,
        [SMEM, SMEM, SMEM, ANY, ANY] + [VMEM] * 5,
        shape((8, 16, 8, LANES), F32),
        VMEM,
        [
            pltpu.VMEM((2, 2, 64, 1024), F32),
            pltpu.VMEM((2, PAIRS, 1024), F32),
            pltpu.SemaphoreType.DMA((2,)),
        ],
        16,
        10**9,
    )(ladder_tiles, cycle_tiles, partner, ladder_total, cycle_total, place, *ladder_moved, *cycle_moved)


def solution(mesh):
    placed = (
        P("pi", "pj", None, "vert"),
        P(None, "vert", None),
        P(),
        P("pj", None, None, "vert"),
        P(),
        P(),
    )
    return jax.shard_map(
        body, mesh=mesh, in_specs=placed, out_specs=P("pi", "pj", None, "vert"), check_vma=False
    )
```

```python
import jax
import jax.numpy as jnp
import numpy as np
from jax import lax
from jax.experimental import pallas as pl
from jax.experimental.pallas import tpu as pltpu
from jax.sharding import PartitionSpec as P

TILE = 64
REACH = 2
BAND = 5
ROWS = 8
LANES = 512
PAIRS = 128
BF = jnp.bfloat16
F32 = jnp.float32
MIB = 1 << 20


def vert_moves(move):
    return [(v, move(v // 4, v % 4)) for v in range(8)]


FLIP = vert_moves(lambda h, y: (1 - h) * 4 + y)
UP = vert_moves(lambda h, y: h * 4 + (y + 1) % 4)
DOWN = vert_moves(lambda h, y: h * 4 + (y + 3) % 4)


def pair_moves(k):
    return [
        (p * 4 + q, (2 * q + ((p % 2) ^ k)) * 4 + p // 2) for p in range(8) for q in range(4)
    ]


def send_order():
    row = np.arange(1024)
    slot, a, v, b = row // 512, (row // 64) % 8, (row // 8) % 8, row % 8
    return v * 128 + slot * 64 + b * 8 + a


def place_order():
    row = np.arange(1024)
    v, slot, b, a = row // 128, (row // 64) % 2, (row // 8) % 8, row % 8
    return slot * 512 + b * 64 + v * 8 + a


def permutation(order):
    columns = lax.broadcasted_iota(jnp.int32, (1024, 1024), 1)
    return (jnp.asarray(order, jnp.int32)[:, None] == columns).astype(BF)


def pick_rows(wanted, amplitudes):
    column = lax.broadcasted_iota(jnp.int32, (256, 128), 1)
    offset = wanted - column
    pick = jnp.concatenate(
        [jnp.where(offset == c * 128, 1.0, 0.0).astype(BF) for c in range(8)], axis=1
    )
    return jnp.dot(pick, amplitudes[...], preferred_element_type=F32).astype(BF)


def cycle_prepare_kernel(tiles, amplitudes, ints, ints_ref, inner_ref, first_ref, last_ref, wide, tall):
    row = lax.broadcasted_iota(jnp.int32, (256, 128), 0)
    i, j, r = row & 7, row >> 4, (row >> 3) & 1
    tile = tiles[0, 1] + r * (tiles[1, 1] - tiles[0, 1])
    inner = pick_rows((i * 16 + j) * 8 + tile, amplitudes).reshape(16, 16, LANES)
    inner_ref[...] = inner
    first_ref[...] = inner[:REACH]
    last_ref[...] = inner[16 - REACH :]
    for t in range(4):
        wide[t] = ints[:, t * 128 : (t + 1) * 128].astype(F32)
    low = lax.broadcasted_iota(jnp.int32, (80, 128), 1) < TILE
    for t in range(4):
        zero = wide[t, pl.ds(0, 80, stride=2), :]
        one = wide[t, pl.ds(1, 80, stride=2), :]
        tall[pl.ds(2 * t, 80, stride=8), :] = jnp.where(low, zero, pltpu.roll(one, TILE, 1))
        tall[pl.ds(2 * t + 1, 80, stride=8), :] = jnp.where(low, pltpu.roll(zero, TILE, 1), one)
    for b in range(4):
        ints_ref[:, b * 128 : (b + 1) * 128] = tall[b * 160 : (b + 1) * 160, :].astype(BF)


def ladder_prepare_kernel(tiles, amplitudes, order, own_ref):
    del order
    row = lax.broadcasted_iota(jnp.int32, (256, 128), 0)
    i, j, w = row & 7, (row >> 3) & 15, row >> 7
    tile = tiles[0, 1] + w * (tiles[1, 1] - tiles[0, 1])
    own_ref[...] = pick_rows((i * 16 + j) * 8 + tile, amplitudes)


def split_pieces(refs, rows):
    own, flip, up, down, up_2, down_2, up_3, down_3 = refs
    vert = lax.axis_index("vert")
    h, y = vert // 4, vert % 4
    half = rows // 2
    pieces = []
    for w in range(2):
        base = w * half
        places = [
            (h, y, own, base), (1 - h, y, flip, base),
            (h, y + 3, up, base), (h, y + 1, down, base),
            (1 - h, y + 3, up_2, base), (1 - h, y + 1, down_2, base),
            (h, y + 2, (up_2, down_2)[w], rows), (1 - h, y + 2, (up_3, down_3)[w], 0),
        ]
        pieces.append([(a * 4 + b % 4, ref, pl.ds(first, half)) for a, b, ref, first in places])
    return pieces


def packed_halves(total, swap):
    parity = lax.axis_index("pi") % 2
    sent = jnp.dot(total[...].astype(BF), swap[...], preferred_element_type=F32).astype(BF)
    upper, under = sent[:64], sent[64:]
    return jnp.where(parity == 0, upper, under), jnp.where(parity == 0, under, upper)


def cycle_kernel(ladder_hbm, before, inner, after, swap, *refs):
    total, first_ref, second_ref, ladder_ints, ints, sem = refs[8:]
    load = pltpu.make_async_copy(ladder_hbm, ladder_ints, sem)
    load.start()
    for w, pieces in enumerate(split_pieces(refs[:8], 160)):
        for source, ref, where in pieces:
            ints[source, w * 80 : (w + 1) * 80, :] = ref[where, :].astype(F32)

    def rows_of(j):
        if j < REACH:
            return before[j]
        if j < REACH + 16:
            return inner[j - REACH]
        return after[j - REACH - 16]

    laid = []
    for j in range(16 + 2 * REACH):
        block = rows_of(j)
        laid.append(
            jnp.concatenate([block[:, a * TILE : (a + 1) * TILE] for a in range(ROWS)], axis=0)
        )
    low = lax.broadcasted_iota(jnp.int32, (8, 128), 1) < TILE
    for j in range(16):
        left = jnp.concatenate([laid[j + o] for o in range(BAND)], axis=1)
        base, lanes = (j % 4) * 40, (j // 4) * 128
        right = jnp.concatenate(
            [
                ints[v, base + o * 8 : base + o * 8 + 8, lanes : lanes + 128]
                for o in range(BAND)
                for v in range(8)
            ],
            axis=0,
        ).astype(BF)
        done = jnp.dot(left, right, preferred_element_type=F32)
        for r in range(2):
            for t in range(4):
                even = done[t * 32 + r * 8 : t * 32 + r * 8 + 8]
                odd = done[t * 32 + 16 + r * 8 : t * 32 + 16 + r * 8 + 8]
                if r == 0:
                    odd = pltpu.roll(odd, TILE, 1)
                else:
                    even = pltpu.roll(even, TILE, 1)
                lane = r * LANES + t * 128
                total[j * 8 : j * 8 + 8, lane : lane + 128] = jnp.where(low, even, odd)
    for half, ref in zip(packed_halves(total, swap), (first_ref, second_ref)):
        for v in range(8):
            ref[v] = half[:, v * 128 : (v + 1) * 128]
    load.wait()


def ladder_kernel(ladder_ints, swap, cycle_0, cycle_1, *refs):
    total, sent_ref = refs[8:]
    for which, pieces in enumerate(split_pieces(refs[:8], 256)):
        acc = None
        for source, ref, where in pieces:
            start = pl.multiple_of(source * LANES, LANES)
            part = lax.dot_general(
                ref[where, :],
                ladder_ints[which, :, pl.ds(start, LANES)],
                (((1,), (1,)), ((), ())),
                preferred_element_type=F32,
            )
            acc = part if acc is None else acc + part
        total[:, which * LANES : (which + 1) * LANES] = acc
    for k, half in enumerate(packed_halves(total, swap)):
        for v in range(8):
            sent_ref[v, k] = half[:, v * 128 : (v + 1) * 128]
    sent_ref[:, 2] = cycle_0[...]
    sent_ref[:, 3] = cycle_1[...]


def finish_kernel(
    ladder_tiles, cycle_tiles, partner, ladder, cycle, place, first, second, arrived, out_ref, mirrored
):
    parity = lax.axis_index("pi") % 2
    for s in range(2):
        for k in range(2):
            if s == 0:
                blocks = [(first, second)[k][v] for v in range(8)]
            else:
                blocks = [arrived[v, 2 + k] for v in range(8)]
            wide = jnp.concatenate(blocks, axis=1)
            mirrored[s, parity ^ k] = jnp.dot(wide, place[...], preferred_element_type=F32)
    dests = [ladder_tiles[0, 0], ladder_tiles[1, 0], cycle_tiles[0, 0], cycle_tiles[1, 0]]
    tile = lax.broadcasted_iota(jnp.int32, (8, LANES), 0)
    own = [(tile == dest).astype(F32) for dest in dests]
    other = [(tile == partner[dest]).astype(F32) for dest in dests]

    def one(i):
        for j in range(16):
            acc = None
            for s in range(4):
                lanes = slice((s % 2) * LANES, (s % 2 + 1) * LANES)
                source = ladder if s < 2 else cycle
                term = own[s] * source[pl.ds(j * 8 + i, 1), lanes]
                acc = term if acc is None else acc + term
                acc = acc + other[s] * mirrored[s // 2, j // 8, pl.ds(i * 8 + j % 8, 1), lanes]
            out_ref[i, j] = acc

    pl.loop(0, 8)(one)


SMEM = pl.BlockSpec(memory_space=pltpu.SMEM)
VMEM = pl.BlockSpec(memory_space=pltpu.VMEM)
ANY = pl.BlockSpec(memory_space=pl.ANY)


def call(kernel, ins, outs, out_specs, scratch, limit, flops):
    return pl.pallas_call(
        kernel,
        out_shape=outs,
        in_specs=ins,
        out_specs=out_specs,
        scratch_shapes=scratch,
        compiler_params=pltpu.CompilerParams(vmem_limit_bytes=limit * MIB),
        cost_estimate=pl.CostEstimate(flops=flops, bytes_accessed=4 * MIB, transcendentals=0),
    )


def shape(dims, kind):
    return jax.ShapeDtypeStruct(dims, kind)


def gather(own):
    rows = own.shape[0]
    half = rows // 2
    flip = lax.ppermute(own, "vert", FLIP)
    up = lax.ppermute(own, "vert", UP)
    down = lax.ppermute(own, "vert", DOWN)
    up_2 = lax.ppermute(jnp.concatenate([flip, up[:half]]), "vert", UP)
    down_2 = lax.ppermute(jnp.concatenate([flip, down[half:]]), "vert", DOWN)
    up_3 = lax.ppermute(up_2[:half], "vert", UP)
    down_3 = lax.ppermute(down_2[half:rows], "vert", DOWN)
    return [own, flip, up, down, up_2, down_2, up_3, down_3]


def to_transposed(blocks):
    return [lax.ppermute(block, ("pi", "pj"), pair_moves(k)) for k, block in enumerate(blocks)]


def body(amplitudes, ladder_ints, ladder_tiles, cycle_ints, cycle_tiles, partner):
    amplitudes = amplitudes.reshape(1024, LANES)
    edge = shape((REACH, 16, LANES), BF)
    ints_own, inner, first, last = call(
        cycle_prepare_kernel,
        [SMEM, VMEM, VMEM],
        [shape((160, LANES), BF), shape((16, 16, LANES), BF), edge, edge],
        [VMEM] * 4,
        [pltpu.VMEM((4, 160, 128), F32), pltpu.VMEM((640, 128), F32)],
        12,
        10**9,
    )(cycle_tiles, amplitudes, cycle_ints.reshape(160, LANES))
    swap, place = permutation(send_order()), permutation(place_order())
    total = shape((PAIRS, 1024), F32)
    block = shape((8, 64, 128), BF)

    ints_pieces = gather(ints_own)
    before = lax.ppermute(last, "pj", [(q, q + 1) for q in range(3)])
    after = lax.ppermute(first, "pj", [(q + 1, q) for q in range(3)])
    ladder_own = call(
        ladder_prepare_kernel, [SMEM, VMEM, ANY], shape((256, LANES), BF), VMEM, [], 8, 10**9
    )(ladder_tiles, amplitudes, ints_pieces[1])
    ladder_pieces = gather(ladder_own)

    cycle_total, *cycle_blocks, ladder_near = call(
        cycle_kernel,
        [ANY] + [VMEM] * 12,
        [total, block, block, shape((2, LANES, 4096), BF)],
        [VMEM] * 4,
        [pltpu.VMEM((8, 160, LANES), F32), pltpu.SemaphoreType.DMA],
        16,
        10**9,
    )(ladder_ints, before, inner, after, swap, *ints_pieces)
    cycle_moved = to_transposed(cycle_blocks)

    ladder_total, sent = call(
        ladder_kernel,
        [VMEM] * 12,
        [total, shape((8, 4, 64, 128), BF)],
        [VMEM] * 2,
        [],
        12,
        2 * 10**9,
    )(ladder_near, swap, *cycle_moved, *ladder_pieces)
    arrived = lax.all_to_all(sent, "vert", 0, 0)
    ladder_moved = to_transposed([arrived[:, 0], arrived[:, 1]])

    return call(
        finish_kernel,
        [SMEM, SMEM, SMEM] + [VMEM] * 6,
        shape((8, 16, 8, LANES), F32),
        VMEM,
        [pltpu.VMEM((2, 2, 64, 1024), F32)],
        12,
        10**9,
    )(ladder_tiles, cycle_tiles, partner, ladder_total, cycle_total, place, *ladder_moved, arrived)


def solution(mesh):
    placed = (
        P("pi", "pj", None, "vert"),
        P(None, "vert", None),
        P(),
        P("pj", None, None, "vert"),
        P(),
        P(),
    )
    return jax.shard_map(
        body, mesh=mesh, in_specs=placed, out_specs=P("pi", "pj", None, "vert"), check_vma=False
    )
```

```python
import jax
import jax.numpy as jnp
import numpy as np
from jax import lax
from jax.experimental import pallas as pl
from jax.experimental.pallas import tpu as pltpu
from jax.sharding import PartitionSpec as P

TILE = 64
REACH = 2
BAND = 5
ROWS = 8
LANES = 512
PAIRS = 128
BF = jnp.bfloat16
F32 = jnp.float32
MIB = 1 << 20


def vert_moves(move):
    return [(v, move(v // 4, v % 4)) for v in range(8)]


FLIP = vert_moves(lambda h, y: (1 - h) * 4 + y)
UP = vert_moves(lambda h, y: h * 4 + (y + 1) % 4)
DOWN = vert_moves(lambda h, y: h * 4 + (y + 3) % 4)


def pair_moves(k):
    return [
        (p * 4 + q, (2 * q + ((p % 2) ^ k)) * 4 + p // 2) for p in range(8) for q in range(4)
    ]


def send_order():
    row = np.arange(1024)
    slot, a, v, b = row // 512, (row // 64) % 8, (row // 8) % 8, row % 8
    return v * 128 + slot * 64 + b * 8 + a


def place_order():
    row = np.arange(1024)
    v, slot, b, a = row // 128, (row // 64) % 2, (row // 8) % 8, row % 8
    return slot * 512 + b * 64 + v * 8 + a


def permutation(order):
    columns = lax.broadcasted_iota(jnp.int32, (1024, 1024), 1)
    return (jnp.asarray(order, jnp.int32)[:, None] == columns).astype(BF)


HALF = 208


def prepare_kernel(
    ladder_tiles, cycle_tiles, amplitudes, ints, own_ref, inner_ref, first_ref, last_ref, wide, tall
):
    row = lax.broadcasted_iota(jnp.int32, (512, 128), 0)
    column = lax.broadcasted_iota(jnp.int32, (512, 128), 1)
    ladder_row = row < 256
    i = row & 7
    j = jnp.where(ladder_row, (row >> 3) & 15, (row >> 4) & 15)
    which = jnp.where(ladder_row, (row >> 7) & 1, (row >> 3) & 1)
    ladder_0, cycle_0 = ladder_tiles[0, 1], cycle_tiles[0, 1]
    tile = jnp.where(
        ladder_row,
        ladder_0 + which * (ladder_tiles[1, 1] - ladder_0),
        cycle_0 + which * (cycle_tiles[1, 1] - cycle_0),
    )
    wanted = (i * 16 + j) * 8 + tile - column
    pick = jnp.concatenate(
        [jnp.where(wanted == c * 128, 1.0, 0.0).astype(BF) for c in range(8)], axis=1
    )
    picked = jnp.dot(pick, amplitudes[...], preferred_element_type=F32).astype(BF)
    for w in range(2):
        own_ref[w * HALF : w * HALF + PAIRS, :] = picked[w * PAIRS : (w + 1) * PAIRS]
    inner = picked[256:].reshape(16, 16, LANES)
    inner_ref[...] = inner
    first_ref[...] = inner[:REACH]
    last_ref[...] = inner[16 - REACH :]
    for t in range(4):
        wide[t] = ints[:, t * 128 : (t + 1) * 128].astype(F32)
    low = lax.broadcasted_iota(jnp.int32, (80, 128), 1) < TILE
    for t in range(4):
        zero = wide[t, pl.ds(0, 80, stride=2), :]
        one = wide[t, pl.ds(1, 80, stride=2), :]
        tall[pl.ds(2 * t, 80, stride=8), :] = jnp.where(low, zero, pltpu.roll(one, TILE, 1))
        tall[pl.ds(2 * t + 1, 80, stride=8), :] = jnp.where(low, pltpu.roll(zero, TILE, 1), one)
    for b in range(4):
        for w in range(2):
            own_ref[w * HALF + PAIRS : (w + 1) * HALF, b * 128 : (b + 1) * 128] = tall[
                b * 160 + w * 80 : b * 160 + (w + 1) * 80, :
            ].astype(BF)


def near_pieces(refs):
    own, flip, up, down = refs
    vert = lax.axis_index("vert")
    h, y = vert // 4, vert % 4
    places = [(h, y, own), (1 - h, y, flip), (h, y + 3, up), (h, y + 1, down)]
    return [[(a * 4 + b % 4, ref, w * HALF) for a, b, ref in places] for w in range(2)]


def far_pieces(refs):
    up_2, down_2, up_3, down_3 = refs
    vert = lax.axis_index("vert")
    h, y = vert // 4, vert % 4
    pieces = []
    for w in range(2):
        places = [
            (1 - h, y + 3, up_2, w * HALF), (1 - h, y + 1, down_2, w * HALF),
            (h, y + 2, (up_2, down_2)[w], 2 * HALF), (1 - h, y + 2, (up_3, down_3)[w], 0),
        ]
        pieces.append([(a * 4 + b % 4, ref, first) for a, b, ref, first in places])
    return pieces


def ladder_part(which, pieces, ladder_ints, acc):
    for source, ref, first in pieces:
        start = pl.multiple_of(source * LANES, LANES)
        part = lax.dot_general(
            ref[first : first + PAIRS, :],
            ladder_ints[which, :, pl.ds(start, LANES)],
            (((1,), (1,)), ((), ())),
            preferred_element_type=F32,
        )
        acc = part if acc is None else acc + part
    return acc


def near_kernel(ladder_ints, *refs):
    for which, pieces in enumerate(near_pieces(refs[:4])):
        refs[4][:, which * LANES : (which + 1) * LANES] = ladder_part(
            which, pieces, ladder_ints, None
        )


def main_kernel(ladder_ints, near, before, inner, after, swap, *refs):
    total, first_ref, second_ref, ints = refs[8:]
    far = far_pieces(refs[4:8])
    for w, pieces in enumerate(near_pieces(refs[:4])):
        for source, ref, first in pieces + far[w]:
            ints[source, w * 80 : (w + 1) * 80, :] = ref[first + PAIRS : first + HALF, :].astype(F32)

    def rows_of(j):
        if j < REACH:
            return before[j]
        if j < REACH + 16:
            return inner[j - REACH]
        return after[j - REACH - 16]

    laid = []
    for j in range(16 + 2 * REACH):
        block = rows_of(j)
        laid.append(
            jnp.concatenate([block[:, a * TILE : (a + 1) * TILE] for a in range(ROWS)], axis=0)
        )
    low = lax.broadcasted_iota(jnp.int32, (8, 128), 1) < TILE
    for j in range(16):
        left = jnp.concatenate([laid[j + o] for o in range(BAND)], axis=1)
        base, lanes = (j % 4) * 40, (j // 4) * 128
        right = jnp.concatenate(
            [
                ints[v, base + o * 8 : base + o * 8 + 8, lanes : lanes + 128]
                for o in range(BAND)
                for v in range(8)
            ],
            axis=0,
        ).astype(BF)
        done = jnp.dot(left, right, preferred_element_type=F32)
        for r in range(2):
            for t in range(4):
                even = done[t * 32 + r * 8 : t * 32 + r * 8 + 8]
                odd = done[t * 32 + 16 + r * 8 : t * 32 + 16 + r * 8 + 8]
                if r == 0:
                    odd = pltpu.roll(odd, TILE, 1)
                else:
                    even = pltpu.roll(even, TILE, 1)
                lane = 1024 + r * LANES + t * 128
                total[j * 8 : j * 8 + 8, lane : lane + 128] = jnp.where(low, even, odd)
    for which in range(2):
        lanes = slice(which * LANES, (which + 1) * LANES)
        total[:, lanes] = ladder_part(which, far[which], ladder_ints, near[:, lanes])
    parity = lax.axis_index("pi") % 2
    for s in range(2):
        sent = jnp.dot(
            total[:, s * 1024 : (s + 1) * 1024].astype(BF), swap[...], preferred_element_type=F32
        ).astype(BF)
        upper, under = sent[:64], sent[64:]
        halves = (jnp.where(parity == 0, upper, under), jnp.where(parity == 0, under, upper))
        for half, ref in zip(halves, (first_ref, second_ref)):
            for v in range(8):
                ref[v, s * 64 : (s + 1) * 64, :] = half[:, v * 128 : (v + 1) * 128]


def finish_kernel(ladder_tiles, cycle_tiles, partner, total, place, first, second, out_ref, mirrored):
    parity = lax.axis_index("pi") % 2
    for k, arrived in enumerate((first, second)):
        wide = jnp.concatenate([arrived[v] for v in range(8)], axis=1)
        moved = jnp.dot(wide, place[...], preferred_element_type=F32)
        for s in range(2):
            mirrored[s, parity ^ k] = moved[s * 64 : (s + 1) * 64]
    dests = [ladder_tiles[0, 0], ladder_tiles[1, 0], cycle_tiles[0, 0], cycle_tiles[1, 0]]
    tile = lax.broadcasted_iota(jnp.int32, (8, LANES), 0)
    own = [(tile == dest).astype(F32) for dest in dests]
    other = [(tile == partner[dest]).astype(F32) for dest in dests]

    def one(i):
        for j in range(16):
            acc = None
            for s in range(4):
                lanes = slice((s % 2) * LANES, (s % 2 + 1) * LANES)
                term = own[s] * total[pl.ds(j * 8 + i, 1), s * LANES : (s + 1) * LANES]
                acc = term if acc is None else acc + term
                acc = acc + other[s] * mirrored[s // 2, j // 8, pl.ds(i * 8 + j % 8, 1), lanes]
            out_ref[i, j] = acc

    pl.loop(0, 8)(one)


SMEM = pl.BlockSpec(memory_space=pltpu.SMEM)
VMEM = pl.BlockSpec(memory_space=pltpu.VMEM)
ANY = pl.BlockSpec(memory_space=pl.ANY)


def call(kernel, ins, outs, out_specs, scratch, limit, flops):
    return pl.pallas_call(
        kernel,
        out_shape=outs,
        in_specs=ins,
        out_specs=out_specs,
        scratch_shapes=scratch,
        compiler_params=pltpu.CompilerParams(vmem_limit_bytes=limit * MIB),
        cost_estimate=pl.CostEstimate(flops=flops, bytes_accessed=4 * MIB, transcendentals=0),
    )


def shape(dims, kind):
    return jax.ShapeDtypeStruct(dims, kind)


def gather(own):
    flip = lax.ppermute(own, "vert", FLIP)
    up = lax.ppermute(own, "vert", UP)
    down = lax.ppermute(own, "vert", DOWN)
    up_2 = lax.ppermute(jnp.concatenate([flip, up[:HALF]]), "vert", UP)
    down_2 = lax.ppermute(jnp.concatenate([flip, down[HALF:]]), "vert", DOWN)
    up_3 = lax.ppermute(up_2[:HALF], "vert", UP)
    down_3 = lax.ppermute(down_2[HALF : 2 * HALF], "vert", DOWN)
    return [own, flip, up, down], [up_2, down_2, up_3, down_3]


def body(amplitudes, ladder_ints, ladder_tiles, cycle_ints, cycle_tiles, partner):
    edge = shape((REACH, 16, LANES), BF)
    own, inner, first, last = call(
        prepare_kernel,
        [SMEM, SMEM, VMEM, VMEM],
        [shape((2 * HALF, LANES), BF), shape((16, 16, LANES), BF), edge, edge],
        [VMEM] * 4,
        [pltpu.VMEM((4, 160, 128), F32), pltpu.VMEM((640, 128), F32)],
        12,
        10**9,
    )(ladder_tiles, cycle_tiles, amplitudes.reshape(1024, LANES), cycle_ints.reshape(160, LANES))
    near, far = gather(own)
    before = lax.ppermute(last, "pj", [(q, q + 1) for q in range(3)])
    after = lax.ppermute(first, "pj", [(q + 1, q) for q in range(3)])
    begun = call(
        near_kernel, [VMEM] * 5, shape((PAIRS, 1024), F32), VMEM, [], 8, 10**9
    )(ladder_ints, *near)
    block = shape((8, 128, 128), BF)
    total, sent_0, sent_1 = call(
        main_kernel,
        [VMEM] * 14,
        [shape((PAIRS, 2048), F32), block, block],
        [VMEM] * 3,
        [pltpu.VMEM((8, 160, LANES), F32)],
        12,
        2 * 10**9,
    )(ladder_ints, begun, before, inner, after, permutation(send_order()), *near, *far)
    moved_0 = lax.ppermute(sent_0, ("pi", "pj"), pair_moves(0))
    arrived_1 = lax.all_to_all(sent_1, "vert", 0, 0)
    arrived_0 = lax.all_to_all(moved_0, "vert", 0, 0)
    moved_1 = lax.ppermute(arrived_1, ("pi", "pj"), pair_moves(1))
    return call(
        finish_kernel,
        [SMEM, SMEM, SMEM] + [VMEM] * 4,
        shape((8, 16, 8, LANES), F32),
        VMEM,
        [pltpu.VMEM((2, 2, 64, 1024), F32)],
        12,
        10**9,
    )(ladder_tiles, cycle_tiles, partner, total, permutation(place_order()), arrived_0, moved_1)


def solution(mesh):
    placed = (
        P("pi", "pj", None, "vert"),
        P(None, "vert", None),
        P(),
        P("pj", None, None, "vert"),
        P(),
        P(),
    )
    return jax.shard_map(
        body, mesh=mesh, in_specs=placed, out_specs=P("pi", "pj", None, "vert"), check_vma=False
    )
```

```python
import jax
import jax.numpy as jnp
import numpy as np
from jax import lax
from jax.experimental import pallas as pl
from jax.experimental.pallas import tpu as pltpu
from jax.sharding import PartitionSpec as P

TILE = 64
REACH = 2
BAND = 5
ROWS = 8
LANES = 512
PAIRS = 128
BF = jnp.bfloat16
F32 = jnp.float32
MIB = 1 << 20


def vert_moves(move):
    return [(v, move(v // 4, v % 4)) for v in range(8)]


FLIP = vert_moves(lambda h, y: (1 - h) * 4 + y)
UP = vert_moves(lambda h, y: h * 4 + (y + 1) % 4)
DOWN = vert_moves(lambda h, y: h * 4 + (y + 3) % 4)


def pair_moves(k):
    return [
        (p * 4 + q, (2 * q + ((p % 2) ^ k)) * 4 + p // 2) for p in range(8) for q in range(4)
    ]


def send_order():
    row = np.arange(1024)
    slot, a, v, b = row // 512, (row // 64) % 8, (row // 8) % 8, row % 8
    return v * 128 + slot * 64 + b * 8 + a


def place_order():
    row = np.arange(1024)
    v, slot, b, a = row // 128, (row // 64) % 2, (row // 8) % 8, row % 8
    return slot * 512 + b * 64 + v * 8 + a


def permutation(order):
    columns = lax.broadcasted_iota(jnp.int32, (1024, 1024), 1)
    return (jnp.asarray(order, jnp.int32)[:, None] == columns).astype(BF)


HALF = 208


def prepare_kernel(*refs):
    inputs, (own_ref, inner_ref, first_ref, last_ref), held = refs[:4], refs[4:8], refs[8:12]
    wide, tall, sems = refs[12:]
    loads = [pltpu.make_async_copy(a, b, sems.at[n]) for n, (a, b) in enumerate(zip(inputs, held))]
    for load in loads:
        load.start()
    ladder_tiles, cycle_tiles, amplitudes, ints = held
    loads[3].wait()
    for n in range(80):
        for t in range(4):
            wide[t, 2 * n : 2 * n + 2, :] = ints[n, :, t * 128 : (t + 1) * 128].astype(F32)
    low = lax.broadcasted_iota(jnp.int32, (80, 128), 1) < TILE
    for t in range(4):
        zero = wide[t, pl.ds(0, 80, stride=2), :]
        one = wide[t, pl.ds(1, 80, stride=2), :]
        tall[pl.ds(2 * t, 80, stride=8), :] = jnp.where(low, zero, pltpu.roll(one, TILE, 1))
        tall[pl.ds(2 * t + 1, 80, stride=8), :] = jnp.where(low, pltpu.roll(zero, TILE, 1), one)
    for b in range(4):
        for w in range(2):
            own_ref[w * HALF + PAIRS : (w + 1) * HALF, b * 128 : (b + 1) * 128] = tall[
                b * 160 + w * 80 : b * 160 + (w + 1) * 80, :
            ].astype(BF)
    row = lax.broadcasted_iota(jnp.int32, (512, 128), 0)
    column = lax.broadcasted_iota(jnp.int32, (512, 128), 1)
    ladder_row = row < 256
    for load in loads[:2]:
        load.wait()
    i = row & 7
    j = jnp.where(ladder_row, (row >> 3) & 15, (row >> 4) & 15)
    which = jnp.where(ladder_row, (row >> 7) & 1, (row >> 3) & 1)
    ladder_0, cycle_0 = ladder_tiles[0, 1], cycle_tiles[0, 1]
    tile = jnp.where(
        ladder_row,
        ladder_0 + which * (ladder_tiles[1, 1] - ladder_0),
        cycle_0 + which * (cycle_tiles[1, 1] - cycle_0),
    )
    wanted = (i * 16 + j) * 8 + tile - column
    pick = jnp.concatenate(
        [jnp.where(wanted == c * 128, 1.0, 0.0).astype(BF) for c in range(8)], axis=1
    )
    loads[2].wait()
    picked = jnp.dot(pick, amplitudes[...], preferred_element_type=F32).astype(BF)
    for w in range(2):
        own_ref[w * HALF : w * HALF + PAIRS, :] = picked[w * PAIRS : (w + 1) * PAIRS]
    inner = picked[256:].reshape(16, 16, LANES)
    inner_ref[...] = inner
    first_ref[...] = inner[:REACH]
    last_ref[...] = inner[16 - REACH :]


def near_pieces(refs):
    own, flip, up, down = refs
    vert = lax.axis_index("vert")
    h, y = vert // 4, vert % 4
    places = [(h, y, own), (1 - h, y, flip), (h, y + 3, up), (h, y + 1, down)]
    return [[(a * 4 + b % 4, ref, w * HALF) for a, b, ref in places] for w in range(2)]


def far_pieces(refs):
    up_2, down_2, side_2, up_3, down_3 = refs
    vert = lax.axis_index("vert")
    h, y = vert // 4, vert % 4
    places = [(1 - h, y + 3), (1 - h, y + 1), (h, y + 2), (1 - h, y + 2)]
    held = [
        [(up_2, 0), (down_2, 0), (up_2, HALF), (down_3, 0)],
        [(side_2, 0), (side_2, HALF), (down_2, HALF), (up_3, 0)],
    ]
    return [
        [(a * 4 + b % 4, ref, first) for (a, b), (ref, first) in zip(places, held[w])]
        for w in range(2)
    ]


def ladder_part(which, pieces, ladder_ints, acc):
    for source, ref, first in pieces:
        start = pl.multiple_of(source * LANES, LANES)
        part = lax.dot_general(
            ref[first : first + PAIRS, :],
            ladder_ints[which, :, pl.ds(start, LANES)],
            (((1,), (1,)), ((), ())),
            preferred_element_type=F32,
        )
        acc = part if acc is None else acc + part
    return acc


def near_kernel(ladder_ints, *refs):
    for which, pieces in enumerate(near_pieces(refs[:4])):
        refs[4][:, which * LANES : (which + 1) * LANES] = ladder_part(
            which, pieces, ladder_ints, None
        )


def main_kernel(ladder_ints, near, before, inner, after, swap, *refs):
    total, first_ref, second_ref, ints = refs[9:]
    far = far_pieces(refs[4:9])
    for w, pieces in enumerate(near_pieces(refs[:4])):
        for source, ref, first in pieces + far[w]:
            ints[source, w * 80 : (w + 1) * 80, :] = ref[first + PAIRS : first + HALF, :].astype(F32)

    def rows_of(j):
        if j < REACH:
            return before[j]
        if j < REACH + 16:
            return inner[j - REACH]
        return after[j - REACH - 16]

    laid = []
    for j in range(16 + 2 * REACH):
        block = rows_of(j)
        laid.append(
            jnp.concatenate([block[:, a * TILE : (a + 1) * TILE] for a in range(ROWS)], axis=0)
        )
    low = lax.broadcasted_iota(jnp.int32, (8, 128), 1) < TILE
    for j in range(16):
        left = jnp.concatenate([laid[j + o] for o in range(BAND)], axis=1)
        base, lanes = (j % 4) * 40, (j // 4) * 128
        right = jnp.concatenate(
            [
                ints[v, base + o * 8 : base + o * 8 + 8, lanes : lanes + 128]
                for o in range(BAND)
                for v in range(8)
            ],
            axis=0,
        ).astype(BF)
        done = jnp.dot(left, right, preferred_element_type=F32)
        for r in range(2):
            for t in range(4):
                even = done[t * 32 + r * 8 : t * 32 + r * 8 + 8]
                odd = done[t * 32 + 16 + r * 8 : t * 32 + 16 + r * 8 + 8]
                if r == 0:
                    odd = pltpu.roll(odd, TILE, 1)
                else:
                    even = pltpu.roll(even, TILE, 1)
                lane = 1024 + r * LANES + t * 128
                total[j * 8 : j * 8 + 8, lane : lane + 128] = jnp.where(low, even, odd)
    for which in range(2):
        lanes = slice(which * LANES, (which + 1) * LANES)
        total[:, lanes] = ladder_part(which, far[which], ladder_ints, near[:, lanes])
    parity = lax.axis_index("pi") % 2
    for s in range(2):
        sent = jnp.dot(
            total[:, s * 1024 : (s + 1) * 1024].astype(BF), swap[...], preferred_element_type=F32
        ).astype(BF)
        upper, under = sent[:64], sent[64:]
        halves = (jnp.where(parity == 0, upper, under), jnp.where(parity == 0, under, upper))
        for half, ref in zip(halves, (first_ref, second_ref)):
            for v in range(8):
                ref[v, s * 64 : (s + 1) * 64, :] = half[:, v * 128 : (v + 1) * 128]


def finish_kernel(
    ladder_tiles, cycle_tiles, partner, total, place, first, second, out_ref, mirrored, held, sems
):
    parity = lax.axis_index("pi") % 2
    for k, arrived in enumerate((first, second)):
        wide = jnp.concatenate([arrived[v] for v in range(8)], axis=1)
        moved = jnp.dot(wide, place[...], preferred_element_type=F32)
        for s in range(2):
            mirrored[s, parity ^ k] = moved[s * 64 : (s + 1) * 64]
    dests = [ladder_tiles[0, 0], ladder_tiles[1, 0], cycle_tiles[0, 0], cycle_tiles[1, 0]]
    tile = lax.broadcasted_iota(jnp.int32, (8, LANES), 0)
    own = [(tile == dest).astype(F32) for dest in dests]
    other = [(tile == partner[dest]).astype(F32) for dest in dests]

    def store(i):
        return pltpu.make_async_copy(held.at[i], out_ref.at[i], sems.at[i])

    def one(i):
        for j in range(16):
            acc = None
            for s in range(4):
                lanes = slice((s % 2) * LANES, (s % 2 + 1) * LANES)
                term = own[s] * total[pl.ds(j * 8 + i, 1), s * LANES : (s + 1) * LANES]
                acc = term if acc is None else acc + term
                acc = acc + other[s] * mirrored[s // 2, j // 8, pl.ds(i * 8 + j % 8, 1), lanes]
            held[i, j] = acc
        store(i).start()

    pl.loop(0, 8)(one)
    pl.loop(0, 8)(lambda i: store(i).wait())


SMEM = pl.BlockSpec(memory_space=pltpu.SMEM)
VMEM = pl.BlockSpec(memory_space=pltpu.VMEM)
HBM = pl.BlockSpec(memory_space=pltpu.HBM)


def call(kernel, ins, outs, out_specs, scratch, limit, flops):
    return pl.pallas_call(
        kernel,
        out_shape=outs,
        in_specs=ins,
        out_specs=out_specs,
        scratch_shapes=scratch,
        compiler_params=pltpu.CompilerParams(vmem_limit_bytes=limit * MIB),
        cost_estimate=pl.CostEstimate(flops=flops, bytes_accessed=4 * MIB, transcendentals=0),
    )


def shape(dims, kind):
    return jax.ShapeDtypeStruct(dims, kind)


def gather(own):
    down = lax.ppermute(own, "vert", DOWN)
    up = lax.ppermute(own, "vert", UP)
    flip = lax.ppermute(own, "vert", FLIP)
    side_2 = lax.ppermute(jnp.concatenate([up[HALF:], down[HALF:]]), "vert", FLIP)
    up_2 = lax.ppermute(jnp.concatenate([flip[:HALF], up[:HALF]]), "vert", UP)
    down_2 = lax.ppermute(jnp.concatenate([flip[:HALF], down[HALF:]]), "vert", DOWN)
    up_3 = lax.ppermute(side_2[:HALF], "vert", UP)
    down_3 = lax.ppermute(down_2[:HALF], "vert", DOWN)
    return [own, flip, up, down], [up_2, down_2, side_2, up_3, down_3]


def body(amplitudes, ladder_ints, ladder_tiles, cycle_ints, cycle_tiles, partner):
    edge = shape((REACH, 16, LANES), BF)
    own, inner, first, last = call(
        prepare_kernel,
        [HBM] * 4,
        [shape((2 * HALF, LANES), BF), shape((16, 16, LANES), BF), edge, edge],
        [VMEM] * 4,
        [
            pltpu.SMEM((2, 2), jnp.int32),
            pltpu.SMEM((2, 2), jnp.int32),
            pltpu.VMEM((1024, LANES), BF),
            pltpu.VMEM((80, 2, LANES), BF),
            pltpu.VMEM((4, 160, 128), F32),
            pltpu.VMEM((640, 128), F32),
            pltpu.SemaphoreType.DMA((4,)),
        ],
        60,
        10**9,
    )(ladder_tiles, cycle_tiles, amplitudes.reshape(1024, LANES), cycle_ints.reshape(80, 2, LANES))
    near, far = gather(own)
    before = lax.ppermute(last, "pj", [(q, q + 1) for q in range(3)])
    after = lax.ppermute(first, "pj", [(q + 1, q) for q in range(3)])
    begun = call(
        near_kernel, [VMEM] * 5, shape((PAIRS, 1024), F32), VMEM, [], 8, 10**9
    )(ladder_ints, *near)
    block = shape((8, 128, 128), BF)
    total, sent_0, sent_1 = call(
        main_kernel,
        [VMEM] * 15,
        [shape((PAIRS, 2048), F32), block, block],
        [VMEM] * 3,
        [pltpu.VMEM((8, 160, LANES), F32)],
        12,
        2 * 10**9,
    )(ladder_ints, begun, before, inner, after, permutation(send_order()), *near, *far)
    moved_0 = lax.ppermute(sent_0, ("pi", "pj"), pair_moves(0))
    arrived_1 = lax.all_to_all(sent_1, "vert", 0, 0)
    arrived_0 = lax.all_to_all(moved_0, "vert", 0, 0)
    moved_1 = lax.ppermute(arrived_1, ("pi", "pj"), pair_moves(1))
    whole = shape((8, 16, 8, LANES), F32)
    return call(
        finish_kernel,
        [SMEM, SMEM, SMEM] + [VMEM] * 4,
        whole,
        HBM,
        [
            pltpu.VMEM((2, 2, 64, 1024), F32),
            pltpu.VMEM((8, 16, 8, LANES), F32),
            pltpu.SemaphoreType.DMA((8,)),
        ],
        12,
        10**9,
    )(ladder_tiles, cycle_tiles, partner, total, permutation(place_order()), arrived_0, moved_1)


def solution(mesh):
    placed = (
        P("pi", "pj", None, "vert"),
        P(None, "vert", None),
        P(),
        P("pj", None, None, "vert"),
        P(),
        P(),
    )
    return jax.shard_map(
        body, mesh=mesh, in_specs=placed, out_specs=P("pi", "pj", None, "vert"), check_vma=False
    )
```

```python
import jax
import jax.numpy as jnp
from jax import lax
from jax.experimental import pallas as pl
from jax.experimental.pallas import tpu as pltpu
from jax.sharding import PartitionSpec as P

TILE = 64
REACH = 2
BAND = 5
ROWS = 8
LANES = 512
PAIRS = 128
BF = jnp.bfloat16
F32 = jnp.float32
MIB = 1 << 20


def vert_moves(move):
    return [(v, move(v // 4, v % 4)) for v in range(8)]


FLIP = vert_moves(lambda h, y: (1 - h) * 4 + y)
UP = vert_moves(lambda h, y: h * 4 + (y + 1) % 4)
DOWN = vert_moves(lambda h, y: h * 4 + (y + 3) % 4)


def pair_moves(k):
    return [
        (p * 4 + q, (2 * q + ((p % 2) ^ k)) * 4 + p // 2) for p in range(8) for q in range(4)
    ]


def orders_kernel(after, swap_ref, place_ref):
    del after
    row = lax.broadcasted_iota(jnp.int32, (1024, 128), 0)
    column = lax.broadcasted_iota(jnp.int32, (1024, 128), 1)
    swap = ((row >> 3) & 7) * 128 + (row >> 9) * 64 + (row & 7) * 8 + ((row >> 6) & 7) - column
    place = ((row >> 6) & 1) * 512 + ((row >> 3) & 7) * 64 + (row >> 7) * 8 + (row & 7) - column
    for order, ref in ((swap, swap_ref), (place, place_ref)):
        for c in range(8):
            ref[:, c * 128 : (c + 1) * 128] = jnp.where(order == c * 128, 1.0, 0.0).astype(BF)


HALF = 208


def prepare_kernel(*refs):
    inputs, (own_ref, inner_ref, first_ref, last_ref), held = refs[:4], refs[4:8], refs[8:12]
    wide, tall, sems = refs[12:]
    loads = [pltpu.make_async_copy(a, b, sems.at[n]) for n, (a, b) in enumerate(zip(inputs, held))]
    for load in loads:
        load.start()
    ladder_tiles, cycle_tiles, amplitudes, ints = held
    loads[3].wait()
    for n in range(80):
        for t in range(4):
            wide[t, 2 * n : 2 * n + 2, :] = ints[n, :, t * 128 : (t + 1) * 128].astype(F32)
    low = lax.broadcasted_iota(jnp.int32, (80, 128), 1) < TILE
    for t in range(4):
        zero = wide[t, pl.ds(0, 80, stride=2), :]
        one = wide[t, pl.ds(1, 80, stride=2), :]
        tall[pl.ds(2 * t, 80, stride=8), :] = jnp.where(low, zero, pltpu.roll(one, TILE, 1))
        tall[pl.ds(2 * t + 1, 80, stride=8), :] = jnp.where(low, pltpu.roll(zero, TILE, 1), one)
    for b in range(4):
        for w in range(2):
            own_ref[w * HALF + PAIRS : (w + 1) * HALF, b * 128 : (b + 1) * 128] = tall[
                b * 160 + w * 80 : b * 160 + (w + 1) * 80, :
            ].astype(BF)
    row = lax.broadcasted_iota(jnp.int32, (512, 128), 0)
    column = lax.broadcasted_iota(jnp.int32, (512, 128), 1)
    ladder_row = row < 256
    for load in loads[:2]:
        load.wait()
    i = row & 7
    j = jnp.where(ladder_row, (row >> 3) & 15, (row >> 4) & 15)
    which = jnp.where(ladder_row, (row >> 7) & 1, (row >> 3) & 1)
    ladder_0, cycle_0 = ladder_tiles[0, 1], cycle_tiles[0, 1]
    tile = jnp.where(
        ladder_row,
        ladder_0 + which * (ladder_tiles[1, 1] - ladder_0),
        cycle_0 + which * (cycle_tiles[1, 1] - cycle_0),
    )
    wanted = (i * 16 + j) * 8 + tile - column
    pick = jnp.concatenate(
        [jnp.where(wanted == c * 128, 1.0, 0.0).astype(BF) for c in range(8)], axis=1
    )
    loads[2].wait()
    picked = jnp.dot(pick, amplitudes[...], preferred_element_type=F32).astype(BF)
    for w in range(2):
        own_ref[w * HALF : w * HALF + PAIRS, :] = picked[w * PAIRS : (w + 1) * PAIRS]
    inner = picked[256:].reshape(16, 16, LANES)
    inner_ref[...] = inner
    first_ref[...] = inner[:REACH]
    last_ref[...] = inner[16 - REACH :]


def near_pieces(refs):
    own, down, up, flip = refs
    vert = lax.axis_index("vert")
    h, y = vert // 4, vert % 4
    places = [(h, y, own), (h, y + 1, down), (h, y + 3, up), (1 - h, y, flip)]
    return [[(a * 4 + b % 4, ref, w * HALF) for a, b, ref in places] for w in range(2)]


def far_pieces(refs):
    up_2, down_2, side_2, up_3, down_3 = refs
    vert = lax.axis_index("vert")
    h, y = vert // 4, vert % 4
    places = [(1 - h, y + 3), (1 - h, y + 1), (h, y + 2), (1 - h, y + 2)]
    held = [
        [(up_2, 0), (down_2, 0), (up_2, HALF), (down_3, 0)],
        [(side_2, 0), (side_2, HALF), (down_2, HALF), (up_3, 0)],
    ]
    return [
        [(a * 4 + b % 4, ref, first) for (a, b), (ref, first) in zip(places, held[w])]
        for w in range(2)
    ]


def ladder_part(which, pieces, ladder_ints, acc):
    for source, ref, first in pieces:
        start = pl.multiple_of(source * LANES, LANES)
        part = lax.dot_general(
            ref[first : first + PAIRS, :],
            ladder_ints[which, :, pl.ds(start, LANES)],
            (((1,), (1,)), ((), ())),
            preferred_element_type=F32,
        )
        acc = part if acc is None else acc + part
    return acc


def near_kernel(ladder_ints, *refs):
    for which, pieces in enumerate(near_pieces(refs[:4])):
        refs[4][:, which * LANES : (which + 1) * LANES] = ladder_part(
            which, pieces, ladder_ints, None
        )


def main_kernel(ladder_ints, near, before, inner, after, swap, *refs):
    total, first_ref, second_ref, ints = refs[9:]
    far = far_pieces(refs[4:9])
    for w, pieces in enumerate(near_pieces(refs[:4])):
        for source, ref, first in pieces + far[w]:
            ints[source, w * 80 : (w + 1) * 80, :] = ref[first + PAIRS : first + HALF, :].astype(F32)

    def rows_of(j):
        if j < REACH:
            return before[j]
        if j < REACH + 16:
            return inner[j - REACH]
        return after[j - REACH - 16]

    laid = []
    for j in range(16 + 2 * REACH):
        block = rows_of(j)
        laid.append(
            jnp.concatenate([block[:, a * TILE : (a + 1) * TILE] for a in range(ROWS)], axis=0)
        )
    low = lax.broadcasted_iota(jnp.int32, (8, 128), 1) < TILE
    for j in range(16):
        left = jnp.concatenate([laid[j + o] for o in range(BAND)], axis=1)
        base, lanes = (j % 4) * 40, (j // 4) * 128
        right = jnp.concatenate(
            [
                ints[v, base + o * 8 : base + o * 8 + 8, lanes : lanes + 128]
                for o in range(BAND)
                for v in range(8)
            ],
            axis=0,
        ).astype(BF)
        done = jnp.dot(left, right, preferred_element_type=F32)
        for r in range(2):
            for t in range(4):
                even = done[t * 32 + r * 8 : t * 32 + r * 8 + 8]
                odd = done[t * 32 + 16 + r * 8 : t * 32 + 16 + r * 8 + 8]
                if r == 0:
                    odd = pltpu.roll(odd, TILE, 1)
                else:
                    even = pltpu.roll(even, TILE, 1)
                lane = 1024 + r * LANES + t * 128
                total[j * 8 : j * 8 + 8, lane : lane + 128] = jnp.where(low, even, odd)
    for which in range(2):
        lanes = slice(which * LANES, (which + 1) * LANES)
        total[:, lanes] = ladder_part(which, far[which], ladder_ints, near[:, lanes])
    parity = lax.axis_index("pi") % 2
    for s in range(2):
        sent = jnp.dot(
            total[:, s * 1024 : (s + 1) * 1024].astype(BF), swap[...], preferred_element_type=F32
        ).astype(BF)
        upper, under = sent[:64], sent[64:]
        halves = (jnp.where(parity == 0, upper, under), jnp.where(parity == 0, under, upper))
        for half, ref in zip(halves, (first_ref, second_ref)):
            for v in range(8):
                ref[v, s * 64 : (s + 1) * 64, :] = half[:, v * 128 : (v + 1) * 128]


def finish_kernel(
    ladder_tiles, cycle_tiles, partner, total, place, first, second, out_ref, mirrored, held, sems
):
    parity = lax.axis_index("pi") % 2
    for k, arrived in enumerate((first, second)):
        wide = jnp.concatenate([arrived[v] for v in range(8)], axis=1)
        moved = jnp.dot(wide, place[...], preferred_element_type=F32)
        for s in range(2):
            mirrored[s, parity ^ k] = moved[s * 64 : (s + 1) * 64]
    dests = [ladder_tiles[0, 0], ladder_tiles[1, 0], cycle_tiles[0, 0], cycle_tiles[1, 0]]
    tile = lax.broadcasted_iota(jnp.int32, (8, LANES), 0)
    own = [(tile == dest).astype(F32) for dest in dests]
    other = [(tile == partner[dest]).astype(F32) for dest in dests]

    def store(i):
        return pltpu.make_async_copy(held.at[i], out_ref.at[i], sems.at[i])

    def one(i):
        for j in range(16):
            acc = None
            for s in range(4):
                lanes = slice((s % 2) * LANES, (s % 2 + 1) * LANES)
                term = own[s] * total[pl.ds(j * 8 + i, 1), s * LANES : (s + 1) * LANES]
                acc = term if acc is None else acc + term
                acc = acc + other[s] * mirrored[s // 2, j // 8, pl.ds(i * 8 + j % 8, 1), lanes]
            held[i, j] = acc
        store(i).start()

    pl.loop(0, 8)(one)
    pl.loop(0, 8)(lambda i: store(i).wait())


SMEM = pl.BlockSpec(memory_space=pltpu.SMEM)
VMEM = pl.BlockSpec(memory_space=pltpu.VMEM)
HBM = pl.BlockSpec(memory_space=pltpu.HBM)


def call(kernel, ins, outs, out_specs, scratch, limit, flops):
    return pl.pallas_call(
        kernel,
        out_shape=outs,
        in_specs=ins,
        out_specs=out_specs,
        scratch_shapes=scratch,
        compiler_params=pltpu.CompilerParams(vmem_limit_bytes=limit * MIB),
        cost_estimate=pl.CostEstimate(flops=flops, bytes_accessed=4 * MIB, transcendentals=0),
    )


def shape(dims, kind):
    return jax.ShapeDtypeStruct(dims, kind)


def gather(own):
    down = lax.ppermute(own, "vert", DOWN)
    up = lax.ppermute(own, "vert", UP)
    flip = lax.ppermute(own, "vert", FLIP)
    side_2 = lax.ppermute(jnp.concatenate([up[HALF:], down[HALF:]]), "vert", FLIP)
    up_2 = lax.ppermute(jnp.concatenate([flip[:HALF], up[:HALF]]), "vert", UP)
    down_2 = lax.ppermute(jnp.concatenate([flip[:HALF], down[HALF:]]), "vert", DOWN)
    up_3 = lax.ppermute(side_2[:HALF], "vert", UP)
    down_3 = lax.ppermute(down_2[:HALF], "vert", DOWN)
    return [own, down, up, flip], [up_2, down_2, side_2, up_3, down_3]


def body(amplitudes, ladder_ints, ladder_tiles, cycle_ints, cycle_tiles, partner):
    edge = shape((REACH, 16, LANES), BF)
    own, inner, first, last = call(
        prepare_kernel,
        [HBM] * 4,
        [shape((2 * HALF, LANES), BF), shape((16, 16, LANES), BF), edge, edge],
        [VMEM] * 4,
        [
            pltpu.SMEM((2, 2), jnp.int32),
            pltpu.SMEM((2, 2), jnp.int32),
            pltpu.VMEM((1024, LANES), BF),
            pltpu.VMEM((80, 2, LANES), BF),
            pltpu.VMEM((4, 160, 128), F32),
            pltpu.VMEM((640, 128), F32),
            pltpu.SemaphoreType.DMA((4,)),
        ],
        60,
        10**9,
    )(ladder_tiles, cycle_tiles, amplitudes.reshape(1024, LANES), cycle_ints.reshape(80, 2, LANES))
    near, far = gather(own)
    before = lax.ppermute(last, "pj", [(q, q + 1) for q in range(3)])
    after = lax.ppermute(first, "pj", [(q + 1, q) for q in range(3)])
    matrix = shape((1024, 1024), BF)
    swap, place = call(orders_kernel, [HBM], [matrix] * 2, [VMEM] * 2, [], 8, 2 * 10**10)(near[1])
    begun = call(
        near_kernel, [VMEM] * 5, shape((PAIRS, 1024), F32), VMEM, [], 8, 10**9
    )(ladder_ints, *near)
    block = shape((8, 128, 128), BF)
    total, sent_0, sent_1 = call(
        main_kernel,
        [VMEM] * 15,
        [shape((PAIRS, 2048), F32), block, block],
        [VMEM] * 3,
        [pltpu.VMEM((8, 160, LANES), F32)],
        12,
        2 * 10**9,
    )(ladder_ints, begun, before, inner, after, swap, *near, *far)
    moved_0 = lax.ppermute(sent_0, ("pi", "pj"), pair_moves(0))
    arrived_1 = lax.all_to_all(sent_1, "vert", 0, 0)
    arrived_0 = lax.all_to_all(moved_0, "vert", 0, 0)
    moved_1 = lax.ppermute(arrived_1, ("pi", "pj"), pair_moves(1))
    whole = shape((8, 16, 8, LANES), F32)
    return call(
        finish_kernel,
        [SMEM, SMEM, SMEM] + [VMEM] * 4,
        whole,
        HBM,
        [
            pltpu.VMEM((2, 2, 64, 1024), F32),
            pltpu.VMEM((8, 16, 8, LANES), F32),
            pltpu.SemaphoreType.DMA((8,)),
        ],
        12,
        10**9,
    )(ladder_tiles, cycle_tiles, partner, total, place, arrived_0, moved_1)


def solution(mesh):
    placed = (
        P("pi", "pj", None, "vert"),
        P(None, "vert", None),
        P(),
        P("pj", None, None, "vert"),
        P(),
        P(),
    )
    return jax.shard_map(
        body, mesh=mesh, in_specs=placed, out_specs=P("pi", "pj", None, "vert"), check_vma=False
    )
```

```python
import jax
import jax.numpy as jnp
import numpy as np
from jax import lax
from jax.experimental import pallas as pl
from jax.experimental.pallas import tpu as pltpu
from jax.sharding import PartitionSpec as P

TILE = 64
REACH = 2
BAND = 5
ROWS = 8
LANES = 512
PAIRS = 128
BF = jnp.bfloat16
F32 = jnp.float32
MIB = 1 << 20


def vert_moves(move):
    return [(v, move(v // 4, v % 4)) for v in range(8)]


FLIP = vert_moves(lambda h, y: (1 - h) * 4 + y)
UP = vert_moves(lambda h, y: h * 4 + (y + 1) % 4)
DOWN = vert_moves(lambda h, y: h * 4 + (y + 3) % 4)


def pair_moves(k):
    return [
        (p * 4 + q, (2 * q + ((p % 2) ^ k)) * 4 + p // 2) for p in range(8) for q in range(4)
    ]


def swap_kernel(after, swap_ref):
    del after
    row = lax.broadcasted_iota(jnp.int32, (1024, 128), 0)
    column = lax.broadcasted_iota(jnp.int32, (1024, 128), 1)
    order = ((row >> 3) & 7) * 128 + (row >> 9) * 64 + (row & 7) * 8 + ((row >> 6) & 7) - column
    for c in range(8):
        swap_ref[:, c * 128 : (c + 1) * 128] = jnp.where(order == c * 128, 1.0, 0.0).astype(BF)


def place_matrix():
    row = np.arange(1024)
    v, slot, b, a = row // 128, (row // 64) % 2, (row // 8) % 8, row % 8
    order = jnp.asarray(slot * 512 + b * 64 + v * 8 + a, jnp.int32)
    columns = lax.broadcasted_iota(jnp.int32, (1024, 1024), 1)
    return (order[:, None] == columns).astype(BF)


def second_stage_kernel(before, after, down, up, flip, up_ref, down_ref, side_ref):
    del before, after
    up_ref[:HALF, :] = flip[:HALF, :]
    up_ref[HALF:, :] = up[:HALF, :]
    down_ref[:HALF, :] = flip[:HALF, :]
    down_ref[HALF:, :] = down[HALF:, :]
    side_ref[:HALF, :] = up[HALF:, :]
    side_ref[HALF:, :] = down[HALF:, :]


HALF = 208


def prepare_kernel(*refs):
    inputs, (own_ref, inner_ref, first_ref, last_ref), held = refs[:4], refs[4:8], refs[8:12]
    wide, tall, sems = refs[12:]
    loads = [pltpu.make_async_copy(a, b, sems.at[n]) for n, (a, b) in enumerate(zip(inputs, held))]
    for load in loads:
        load.start()
    ladder_tiles, cycle_tiles, amplitudes, ints = held
    loads[3].wait()
    for n in range(80):
        for t in range(4):
            wide[t, 2 * n : 2 * n + 2, :] = ints[n, :, t * 128 : (t + 1) * 128].astype(F32)
    low = lax.broadcasted_iota(jnp.int32, (80, 128), 1) < TILE
    for t in range(4):
        zero = wide[t, pl.ds(0, 80, stride=2), :]
        one = wide[t, pl.ds(1, 80, stride=2), :]
        tall[pl.ds(2 * t, 80, stride=8), :] = jnp.where(low, zero, pltpu.roll(one, TILE, 1))
        tall[pl.ds(2 * t + 1, 80, stride=8), :] = jnp.where(low, pltpu.roll(zero, TILE, 1), one)
    for b in range(4):
        for w in range(2):
            own_ref[w * HALF + PAIRS : (w + 1) * HALF, b * 128 : (b + 1) * 128] = tall[
                b * 160 + w * 80 : b * 160 + (w + 1) * 80, :
            ].astype(BF)
    row = lax.broadcasted_iota(jnp.int32, (512, 128), 0)
    column = lax.broadcasted_iota(jnp.int32, (512, 128), 1)
    ladder_row = row < 256
    for load in loads[:2]:
        load.wait()
    i = row & 7
    j = jnp.where(ladder_row, (row >> 3) & 15, (row >> 4) & 15)
    which = jnp.where(ladder_row, (row >> 7) & 1, (row >> 3) & 1)
    ladder_0, cycle_0 = ladder_tiles[0, 1], cycle_tiles[0, 1]
    tile = jnp.where(
        ladder_row,
        ladder_0 + which * (ladder_tiles[1, 1] - ladder_0),
        cycle_0 + which * (cycle_tiles[1, 1] - cycle_0),
    )
    wanted = (i * 16 + j) * 8 + tile - column
    pick = jnp.concatenate(
        [jnp.where(wanted == c * 128, 1.0, 0.0).astype(BF) for c in range(8)], axis=1
    )
    loads[2].wait()
    picked = jnp.dot(pick, amplitudes[...], preferred_element_type=F32).astype(BF)
    for w in range(2):
        own_ref[w * HALF : w * HALF + PAIRS, :] = picked[w * PAIRS : (w + 1) * PAIRS]
    inner = picked[256:].reshape(16, 16, LANES)
    inner_ref[...] = inner
    first_ref[...] = inner[:REACH]
    last_ref[...] = inner[16 - REACH :]


def near_pieces(refs):
    own, down, up, flip = refs
    vert = lax.axis_index("vert")
    h, y = vert // 4, vert % 4
    places = [(h, y, own), (h, y + 1, down), (h, y + 3, up), (1 - h, y, flip)]
    return [[(a * 4 + b % 4, ref, w * HALF) for a, b, ref in places] for w in range(2)]


def far_pieces(refs):
    up_2, down_2, side_2, up_3, down_3 = refs
    vert = lax.axis_index("vert")
    h, y = vert // 4, vert % 4
    places = [(1 - h, y + 3), (1 - h, y + 1), (h, y + 2), (1 - h, y + 2)]
    held = [
        [(up_2, 0), (down_2, 0), (up_2, HALF), (down_3, 0)],
        [(side_2, 0), (side_2, HALF), (down_2, HALF), (up_3, 0)],
    ]
    return [
        [(a * 4 + b % 4, ref, first) for (a, b), (ref, first) in zip(places, held[w])]
        for w in range(2)
    ]


def ladder_part(which, pieces, ladder_ints, acc):
    for source, ref, first in pieces:
        start = pl.multiple_of(source * LANES, LANES)
        part = lax.dot_general(
            ref[first : first + PAIRS, :],
            ladder_ints[which, :, pl.ds(start, LANES)],
            (((1,), (1,)), ((), ())),
            preferred_element_type=F32,
        )
        acc = part if acc is None else acc + part
    return acc


def near_kernel(ladder_ints, *refs):
    for which, pieces in enumerate(near_pieces(refs[:4])):
        refs[4][:, which * LANES : (which + 1) * LANES] = ladder_part(
            which, pieces, ladder_ints, None
        )


def main_kernel(ladder_ints, near, before, inner, after, swap, *refs):
    total, first_ref, second_ref, ints = refs[9:]
    far = far_pieces(refs[4:9])
    for w, pieces in enumerate(near_pieces(refs[:4])):
        for source, ref, first in pieces + far[w]:
            ints[source, w * 80 : (w + 1) * 80, :] = ref[first + PAIRS : first + HALF, :].astype(F32)

    def rows_of(j):
        if j < REACH:
            return before[j]
        if j < REACH + 16:
            return inner[j - REACH]
        return after[j - REACH - 16]

    laid = []
    for j in range(16 + 2 * REACH):
        block = rows_of(j)
        laid.append(
            jnp.concatenate([block[:, a * TILE : (a + 1) * TILE] for a in range(ROWS)], axis=0)
        )
    low = lax.broadcasted_iota(jnp.int32, (8, 128), 1) < TILE
    for j in range(16):
        left = jnp.concatenate([laid[j + o] for o in range(BAND)], axis=1)
        base, lanes = (j % 4) * 40, (j // 4) * 128
        right = jnp.concatenate(
            [
                ints[v, base + o * 8 : base + o * 8 + 8, lanes : lanes + 128]
                for o in range(BAND)
                for v in range(8)
            ],
            axis=0,
        ).astype(BF)
        done = jnp.dot(left, right, preferred_element_type=F32)
        for r in range(2):
            for t in range(4):
                even = done[t * 32 + r * 8 : t * 32 + r * 8 + 8]
                odd = done[t * 32 + 16 + r * 8 : t * 32 + 16 + r * 8 + 8]
                if r == 0:
                    odd = pltpu.roll(odd, TILE, 1)
                else:
                    even = pltpu.roll(even, TILE, 1)
                lane = 1024 + r * LANES + t * 128
                total[j * 8 : j * 8 + 8, lane : lane + 128] = jnp.where(low, even, odd)
    for which in range(2):
        lanes = slice(which * LANES, (which + 1) * LANES)
        total[:, lanes] = ladder_part(which, far[which], ladder_ints, near[:, lanes])
    parity = lax.axis_index("pi") % 2
    for s in range(2):
        sent = jnp.dot(
            total[:, s * 1024 : (s + 1) * 1024].astype(BF), swap[...], preferred_element_type=F32
        ).astype(BF)
        upper, under = sent[:64], sent[64:]
        halves = (jnp.where(parity == 0, upper, under), jnp.where(parity == 0, under, upper))
        for half, ref in zip(halves, (first_ref, second_ref)):
            for v in range(8):
                ref[v, s * 64 : (s + 1) * 64, :] = half[:, v * 128 : (v + 1) * 128]


def finish_kernel(
    ladder_tiles, cycle_tiles, partner, total, place, first, second, out_ref, mirrored, held, sems
):
    parity = lax.axis_index("pi") % 2
    for k, arrived in enumerate((first, second)):
        wide = jnp.concatenate([arrived[v] for v in range(8)], axis=1)
        moved = jnp.dot(wide, place[...], preferred_element_type=F32)
        for s in range(2):
            mirrored[s, parity ^ k] = moved[s * 64 : (s + 1) * 64]
    dests = [ladder_tiles[0, 0], ladder_tiles[1, 0], cycle_tiles[0, 0], cycle_tiles[1, 0]]
    tile = lax.broadcasted_iota(jnp.int32, (8, LANES), 0)
    own = [(tile == dest).astype(F32) for dest in dests]
    other = [(tile == partner[dest]).astype(F32) for dest in dests]

    def store(i):
        return pltpu.make_async_copy(held.at[i], out_ref.at[i], sems.at[i])

    def one(i):
        for j in range(16):
            acc = None
            for s in range(4):
                lanes = slice((s % 2) * LANES, (s % 2 + 1) * LANES)
                term = own[s] * total[pl.ds(j * 8 + i, 1), s * LANES : (s + 1) * LANES]
                acc = term if acc is None else acc + term
                acc = acc + other[s] * mirrored[s // 2, j // 8, pl.ds(i * 8 + j % 8, 1), lanes]
            held[i, j] = acc
        store(i).start()

    pl.loop(0, 8)(one)
    pl.loop(0, 8)(lambda i: store(i).wait())


SMEM = pl.BlockSpec(memory_space=pltpu.SMEM)
VMEM = pl.BlockSpec(memory_space=pltpu.VMEM)
HBM = pl.BlockSpec(memory_space=pltpu.HBM)


def call(kernel, ins, outs, out_specs, scratch, limit, flops):
    return pl.pallas_call(
        kernel,
        out_shape=outs,
        in_specs=ins,
        out_specs=out_specs,
        scratch_shapes=scratch,
        compiler_params=pltpu.CompilerParams(vmem_limit_bytes=limit * MIB),
        cost_estimate=pl.CostEstimate(flops=flops, bytes_accessed=4 * MIB, transcendentals=0),
    )


def shape(dims, kind):
    return jax.ShapeDtypeStruct(dims, kind)


def gather(own, before, after):
    down = lax.ppermute(own, "vert", DOWN)
    up = lax.ppermute(own, "vert", UP)
    flip = lax.ppermute(own, "vert", FLIP)
    near = [down, up, flip]
    to_up, to_down, to_side = call(
        second_stage_kernel,
        [HBM] * 2 + [VMEM] * 3,
        [shape((2 * HALF, LANES), BF)] * 3,
        [VMEM] * 3,
        [],
        8,
        10**7,
    )(before, after, *near)
    side_2 = lax.ppermute(to_side, "vert", FLIP)
    up_2 = lax.ppermute(to_up, "vert", UP)
    down_2 = lax.ppermute(to_down, "vert", DOWN)
    up_3 = lax.ppermute(side_2[:HALF], "vert", UP)
    down_3 = lax.ppermute(down_2[:HALF], "vert", DOWN)
    return [own] + near, [up_2, down_2, side_2, up_3, down_3]


def body(amplitudes, ladder_ints, ladder_tiles, cycle_ints, cycle_tiles, partner):
    edge = shape((REACH, 16, LANES), BF)
    own, inner, first, last = call(
        prepare_kernel,
        [HBM] * 4,
        [shape((2 * HALF, LANES), BF), shape((16, 16, LANES), BF), edge, edge],
        [VMEM] * 4,
        [
            pltpu.SMEM((2, 2), jnp.int32),
            pltpu.SMEM((2, 2), jnp.int32),
            pltpu.VMEM((1024, LANES), BF),
            pltpu.VMEM((80, 2, LANES), BF),
            pltpu.VMEM((4, 160, 128), F32),
            pltpu.VMEM((640, 128), F32),
            pltpu.SemaphoreType.DMA((4,)),
        ],
        60,
        10**9,
    )(ladder_tiles, cycle_tiles, amplitudes.reshape(1024, LANES), cycle_ints.reshape(80, 2, LANES))
    before = lax.ppermute(last, "pj", [(q, q + 1) for q in range(3)])
    after = lax.ppermute(first, "pj", [(q + 1, q) for q in range(3)])
    near, far = gather(own, before, after)
    swap = call(
        swap_kernel, [HBM], shape((1024, 1024), BF), VMEM, [], 8, 2 * 10**10
    )(near[1])
    begun = call(
        near_kernel, [VMEM] * 5, shape((PAIRS, 1024), F32), VMEM, [], 8, 10**9
    )(ladder_ints, *near)
    block = shape((8, 128, 128), BF)
    total, sent_0, sent_1 = call(
        main_kernel,
        [VMEM] * 15,
        [shape((PAIRS, 2048), F32), block, block],
        [VMEM] * 3,
        [pltpu.VMEM((8, 160, LANES), F32)],
        12,
        2 * 10**9,
    )(ladder_ints, begun, before, inner, after, swap, *near, *far)
    moved_0 = lax.ppermute(sent_0, ("pi", "pj"), pair_moves(0))
    arrived_1 = lax.all_to_all(sent_1, "vert", 0, 0)
    arrived_0 = lax.all_to_all(moved_0, "vert", 0, 0)
    moved_1 = lax.ppermute(arrived_1, ("pi", "pj"), pair_moves(1))
    whole = shape((8, 16, 8, LANES), F32)
    return call(
        finish_kernel,
        [SMEM, SMEM, SMEM] + [VMEM] * 4,
        whole,
        HBM,
        [
            pltpu.VMEM((2, 2, 64, 1024), F32),
            pltpu.VMEM((8, 16, 8, LANES), F32),
            pltpu.SemaphoreType.DMA((8,)),
        ],
        12,
        10**9,
    )(ladder_tiles, cycle_tiles, partner, total, place_matrix(), arrived_0, moved_1)


def solution(mesh):
    placed = (
        P("pi", "pj", None, "vert"),
        P(None, "vert", None),
        P(),
        P("pj", None, None, "vert"),
        P(),
        P(),
    )
    return jax.shard_map(
        body, mesh=mesh, in_specs=placed, out_specs=P("pi", "pj", None, "vert"), check_vma=False
    )
```

```python
import jax
import jax.numpy as jnp
import numpy as np
from jax import lax
from jax.experimental import pallas as pl
from jax.experimental.pallas import tpu as pltpu
from jax.sharding import PartitionSpec as P

TILE = 64
REACH = 2
BAND = 5
ROWS = 8
LANES = 512
PAIRS = 128
BF = jnp.bfloat16
F32 = jnp.float32
MIB = 1 << 20


def vert_moves(move):
    return [(v, move(v // 4, v % 4)) for v in range(8)]


FLIP = vert_moves(lambda h, y: (1 - h) * 4 + y)
UP = vert_moves(lambda h, y: h * 4 + (y + 1) % 4)
DOWN = vert_moves(lambda h, y: h * 4 + (y + 3) % 4)


def pair_moves(k, dx):
    return [
        ((p * 4 + q) * 8 + v, ((2 * q + ((p % 2) ^ k)) * 4 + p // 2) * 8 + (v ^ (4 * dx)))
        for p in range(8)
        for q in range(4)
        for v in range(8)
    ]


def to_transposed(block, k, dx):
    return lax.ppermute(block, ("pi", "pj", "vert"), pair_moves(k, dx))


def along_y(block, dy):
    return lax.ppermute(block, "vert", vert_moves(lambda h, y: h * 4 + (y + dy) % 4))


def peers(sign):
    vert = lax.axis_index("vert")
    h, y = vert // 4, vert % 4
    found = []
    for dx in range(2):
        for dy in range(4):
            there = (h if dx == 0 else 1 - h) * 4 + (y + (dy if sign > 0 else 4 - dy)) % 4
            found.append((dx, dy, pl.multiple_of(there * 128, 128)))
    return found


def split_kernel(same, other, first, second, third):
    for dy, ref in enumerate((first, second, third), 1):
        ref[0] = same[dy]
        ref[1] = other[dy]


def join_kernel(own, first, second, third, same, other):
    for dy, ref in enumerate((own, first, second, third)):
        same[dy] = ref[0]
        other[dy] = ref[1]


def swap_kernel(after, swap_ref):
    del after
    row = lax.broadcasted_iota(jnp.int32, (1024, 128), 0)
    column = lax.broadcasted_iota(jnp.int32, (1024, 128), 1)
    order = ((row >> 3) & 7) * 128 + (row >> 9) * 64 + (row & 7) * 8 + ((row >> 6) & 7) - column
    for c in range(8):
        swap_ref[:, c * 128 : (c + 1) * 128] = jnp.where(order == c * 128, 1.0, 0.0).astype(BF)


def place_matrix():
    row = np.arange(1024)
    v, slot, b, a = row // 128, (row // 64) % 2, (row // 8) % 8, row % 8
    order = jnp.asarray(slot * 512 + b * 64 + v * 8 + a, jnp.int32)
    columns = lax.broadcasted_iota(jnp.int32, (1024, 1024), 1)
    return (order[:, None] == columns).astype(BF)


def second_stage_kernel(before, after, down, up, flip, up_ref, down_ref, side_ref):
    del before, after
    up_ref[:HALF, :] = flip[:HALF, :]
    up_ref[HALF:, :] = up[:HALF, :]
    down_ref[:HALF, :] = flip[:HALF, :]
    down_ref[HALF:, :] = down[HALF:, :]
    side_ref[:HALF, :] = up[HALF:, :]
    side_ref[HALF:, :] = down[HALF:, :]


HALF = 208


def prepare_kernel(*refs):
    inputs, (own_ref, inner_ref, first_ref, last_ref), held = refs[:4], refs[4:8], refs[8:12]
    wide, tall, sems = refs[12:]
    loads = [pltpu.make_async_copy(a, b, sems.at[n]) for n, (a, b) in enumerate(zip(inputs, held))]
    for load in loads:
        load.start()
    ladder_tiles, cycle_tiles, amplitudes, ints = held
    loads[3].wait()
    for n in range(80):
        for t in range(4):
            wide[t, 2 * n : 2 * n + 2, :] = ints[n, :, t * 128 : (t + 1) * 128].astype(F32)
    low = lax.broadcasted_iota(jnp.int32, (80, 128), 1) < TILE
    for t in range(4):
        zero = wide[t, pl.ds(0, 80, stride=2), :]
        one = wide[t, pl.ds(1, 80, stride=2), :]
        tall[pl.ds(2 * t, 80, stride=8), :] = jnp.where(low, zero, pltpu.roll(one, TILE, 1))
        tall[pl.ds(2 * t + 1, 80, stride=8), :] = jnp.where(low, pltpu.roll(zero, TILE, 1), one)
    for b in range(4):
        for w in range(2):
            own_ref[w * HALF + PAIRS : (w + 1) * HALF, b * 128 : (b + 1) * 128] = tall[
                b * 160 + w * 80 : b * 160 + (w + 1) * 80, :
            ].astype(BF)
    row = lax.broadcasted_iota(jnp.int32, (512, 128), 0)
    column = lax.broadcasted_iota(jnp.int32, (512, 128), 1)
    ladder_row = row < 256
    for load in loads[:2]:
        load.wait()
    i = row & 7
    j = jnp.where(ladder_row, (row >> 3) & 15, (row >> 4) & 15)
    which = jnp.where(ladder_row, (row >> 7) & 1, (row >> 3) & 1)
    ladder_0, cycle_0 = ladder_tiles[0, 1], cycle_tiles[0, 1]
    tile = jnp.where(
        ladder_row,
        ladder_0 + which * (ladder_tiles[1, 1] - ladder_0),
        cycle_0 + which * (cycle_tiles[1, 1] - cycle_0),
    )
    wanted = (i * 16 + j) * 8 + tile - column
    pick = jnp.concatenate(
        [jnp.where(wanted == c * 128, 1.0, 0.0).astype(BF) for c in range(8)], axis=1
    )
    loads[2].wait()
    picked = jnp.dot(pick, amplitudes[...], preferred_element_type=F32).astype(BF)
    for w in range(2):
        own_ref[w * HALF : w * HALF + PAIRS, :] = picked[w * PAIRS : (w + 1) * PAIRS]
    inner = picked[256:].reshape(16, 16, LANES)
    inner_ref[...] = inner
    first_ref[...] = inner[:REACH]
    last_ref[...] = inner[16 - REACH :]


def near_pieces(refs):
    own, down, up, flip = refs
    vert = lax.axis_index("vert")
    h, y = vert // 4, vert % 4
    places = [(h, y, own), (h, y + 1, down), (h, y + 3, up), (1 - h, y, flip)]
    return [[(a * 4 + b % 4, ref, w * HALF) for a, b, ref in places] for w in range(2)]


def far_pieces(refs):
    up_2, down_2, side_2, up_3, down_3 = refs
    vert = lax.axis_index("vert")
    h, y = vert // 4, vert % 4
    places = [(1 - h, y + 3), (1 - h, y + 1), (h, y + 2), (1 - h, y + 2)]
    held = [
        [(up_2, 0), (down_2, 0), (up_2, HALF), (down_3, 0)],
        [(side_2, 0), (side_2, HALF), (down_2, HALF), (up_3, 0)],
    ]
    return [
        [(a * 4 + b % 4, ref, first) for (a, b), (ref, first) in zip(places, held[w])]
        for w in range(2)
    ]


def ladder_part(which, pieces, ladder_ints, acc):
    for source, ref, first in pieces:
        start = pl.multiple_of(source * LANES, LANES)
        part = lax.dot_general(
            ref[first : first + PAIRS, :],
            ladder_ints[which, :, pl.ds(start, LANES)],
            (((1,), (1,)), ((), ())),
            preferred_element_type=F32,
        )
        acc = part if acc is None else acc + part
    return acc


def near_kernel(ladder_ints, *refs):
    for which, pieces in enumerate(near_pieces(refs[:4])):
        refs[4][:, which * LANES : (which + 1) * LANES] = ladder_part(
            which, pieces, ladder_ints, None
        )


def main_kernel(ladder_ints, near, before, inner, after, swap, *refs):
    total, same_ref, other_ref, *late_refs, ints, lanes_buf = refs[9:]
    far = far_pieces(refs[4:9])
    for w, pieces in enumerate(near_pieces(refs[:4])):
        for source, ref, first in pieces + far[w]:
            ints[source, w * 80 : (w + 1) * 80, :] = ref[first + PAIRS : first + HALF, :].astype(F32)

    def rows_of(j):
        if j < REACH:
            return before[j]
        if j < REACH + 16:
            return inner[j - REACH]
        return after[j - REACH - 16]

    laid = []
    for j in range(16 + 2 * REACH):
        block = rows_of(j)
        laid.append(
            jnp.concatenate([block[:, a * TILE : (a + 1) * TILE] for a in range(ROWS)], axis=0)
        )
    low = lax.broadcasted_iota(jnp.int32, (8, 128), 1) < TILE
    for j in range(16):
        left = jnp.concatenate([laid[j + o] for o in range(BAND)], axis=1)
        base, lanes = (j % 4) * 40, (j // 4) * 128
        right = jnp.concatenate(
            [
                ints[v, base + o * 8 : base + o * 8 + 8, lanes : lanes + 128]
                for o in range(BAND)
                for v in range(8)
            ],
            axis=0,
        ).astype(BF)
        done = jnp.dot(left, right, preferred_element_type=F32)
        for r in range(2):
            for t in range(4):
                even = done[t * 32 + r * 8 : t * 32 + r * 8 + 8]
                odd = done[t * 32 + 16 + r * 8 : t * 32 + 16 + r * 8 + 8]
                if r == 0:
                    odd = pltpu.roll(odd, TILE, 1)
                else:
                    even = pltpu.roll(even, TILE, 1)
                lane = 1024 + r * LANES + t * 128
                total[j * 8 : j * 8 + 8, lane : lane + 128] = jnp.where(low, even, odd)
    for which in range(2):
        lanes = slice(which * LANES, (which + 1) * LANES)
        total[:, lanes] = ladder_part(which, far[which], ladder_ints, near[:, lanes])
    both = jnp.concatenate([total[:, :1024], total[:, 1024:]], axis=0).astype(BF)
    lanes_buf[...] = jnp.dot(both, swap[...], preferred_element_type=F32).astype(BF)
    parity = lax.axis_index("pi") % 2
    for s in range(2):
        early = pl.ds(pl.multiple_of(s * 128 + parity * 64, 64), 64)
        late = pl.ds(pl.multiple_of(s * 128 + (1 - parity) * 64, 64), 64)
        rows = slice(s * 64, (s + 1) * 64)
        for dx, dy, start in peers(1):
            (same_ref, other_ref)[dx][dy, rows, :] = lanes_buf[early, pl.ds(start, 128)]
            late_refs[dy][dx, rows, :] = lanes_buf[late, pl.ds(start, 128)]


def finish_kernel(ladder_tiles, cycle_tiles, partner, total, place, *refs):
    arrived, (out_ref, mirrored, wide, held, sems) = refs[:7], refs[7:]
    parity = lax.axis_index("pi") % 2
    for dx, dy, start in peers(-1):
        early = arrived[dx][0] if dy == 0 else arrived[1 + dy][dx]
        wide[:128, pl.ds(start, 128)] = early
        wide[128:, pl.ds(start, 128)] = arrived[5 + dx][dy]
    moved = jnp.dot(wide[...], place[...], preferred_element_type=F32)
    for k in range(2):
        for s in range(2):
            mirrored[s, parity ^ k] = moved[k * 128 + s * 64 : k * 128 + (s + 1) * 64]
    dests = [ladder_tiles[0, 0], ladder_tiles[1, 0], cycle_tiles[0, 0], cycle_tiles[1, 0]]
    tile = lax.broadcasted_iota(jnp.int32, (8, LANES), 0)
    own = [(tile == dest).astype(F32) for dest in dests]
    other = [(tile == partner[dest]).astype(F32) for dest in dests]

    def store(i):
        return pltpu.make_async_copy(held.at[i], out_ref.at[i], sems.at[i])

    def one(i):
        for j in range(16):
            acc = None
            for s in range(4):
                lanes = slice((s % 2) * LANES, (s % 2 + 1) * LANES)
                term = own[s] * total[pl.ds(j * 8 + i, 1), s * LANES : (s + 1) * LANES]
                acc = term if acc is None else acc + term
                acc = acc + other[s] * mirrored[s // 2, j // 8, pl.ds(i * 8 + j % 8, 1), lanes]
            held[i, j] = acc
        store(i).start()

    pl.loop(0, 8)(one)
    pl.loop(0, 8)(lambda i: store(i).wait())


SMEM = pl.BlockSpec(memory_space=pltpu.SMEM)
VMEM = pl.BlockSpec(memory_space=pltpu.VMEM)
HBM = pl.BlockSpec(memory_space=pltpu.HBM)


def call(kernel, ins, outs, out_specs, scratch, limit, flops):
    return pl.pallas_call(
        kernel,
        out_shape=outs,
        in_specs=ins,
        out_specs=out_specs,
        scratch_shapes=scratch,
        compiler_params=pltpu.CompilerParams(vmem_limit_bytes=limit * MIB),
        cost_estimate=pl.CostEstimate(flops=flops, bytes_accessed=4 * MIB, transcendentals=0),
    )


def shape(dims, kind):
    return jax.ShapeDtypeStruct(dims, kind)


def gather(own, before, after):
    down = lax.ppermute(own, "vert", DOWN)
    up = lax.ppermute(own, "vert", UP)
    flip = lax.ppermute(own, "vert", FLIP)
    near = [down, up, flip]
    to_up, to_down, to_side = call(
        second_stage_kernel,
        [HBM] * 2 + [VMEM] * 3,
        [shape((2 * HALF, LANES), BF)] * 3,
        [VMEM] * 3,
        [],
        8,
        10**7,
    )(before, after, *near)
    side_2 = lax.ppermute(to_side, "vert", FLIP)
    up_2 = lax.ppermute(to_up, "vert", UP)
    down_2 = lax.ppermute(to_down, "vert", DOWN)
    up_3 = lax.ppermute(side_2[:HALF], "vert", UP)
    down_3 = lax.ppermute(down_2[:HALF], "vert", DOWN)
    return [own] + near, [up_2, down_2, side_2, up_3, down_3]


def body(amplitudes, ladder_ints, ladder_tiles, cycle_ints, cycle_tiles, partner):
    edge = shape((REACH, 16, LANES), BF)
    own, inner, first, last = call(
        prepare_kernel,
        [HBM] * 4,
        [shape((2 * HALF, LANES), BF), shape((16, 16, LANES), BF), edge, edge],
        [VMEM] * 4,
        [
            pltpu.SMEM((2, 2), jnp.int32),
            pltpu.SMEM((2, 2), jnp.int32),
            pltpu.VMEM((1024, LANES), BF),
            pltpu.VMEM((80, 2, LANES), BF),
            pltpu.VMEM((4, 160, 128), F32),
            pltpu.VMEM((640, 128), F32),
            pltpu.SemaphoreType.DMA((4,)),
        ],
        60,
        10**9,
    )(ladder_tiles, cycle_tiles, amplitudes.reshape(1024, LANES), cycle_ints.reshape(80, 2, LANES))
    before = lax.ppermute(last, "pj", [(q, q + 1) for q in range(3)])
    after = lax.ppermute(first, "pj", [(q + 1, q) for q in range(3)])
    near, far = gather(own, before, after)
    swap = call(
        swap_kernel, [HBM], shape((1024, 1024), BF), VMEM, [], 8, 2 * 10**10
    )(near[1])
    begun = call(
        near_kernel, [VMEM] * 5, shape((PAIRS, 1024), F32), VMEM, [], 8, 10**9
    )(ladder_ints, *near)
    four, two = shape((4, 128, 128), BF), shape((2, 128, 128), BF)
    total, same, other, late_0, late_1, late_2, late_3 = call(
        main_kernel,
        [VMEM] * 15,
        [shape((PAIRS, 2048), F32), four, four, two, two, two, two],
        [VMEM] * 7,
        [pltpu.VMEM((8, 160, LANES), F32), pltpu.VMEM((256, 1024), BF)],
        12,
        2 * 10**9,
    )(ladder_ints, begun, before, inner, after, swap, *near, *far)
    same, other = to_transposed(same, 0, 0), to_transposed(other, 0, 1)
    late = [along_y(block, dy) for dy, block in ((1, late_1), (2, late_2), (3, late_3))]
    joined = call(join_kernel, [VMEM] * 4, [four] * 2, [VMEM] * 2, [], 4, 10**7)(late_0, *late)
    joined = [to_transposed(block, 1, dx) for dx, block in enumerate(joined)]
    early = call(split_kernel, [VMEM] * 2, [two] * 3, [VMEM] * 3, [], 4, 10**7)(same, other)
    early = [along_y(block, dy) for dy, block in enumerate(early, 1)]
    return call(
        finish_kernel,
        [SMEM, SMEM, SMEM] + [VMEM] * 9,
        shape((8, 16, 8, LANES), F32),
        HBM,
        [
            pltpu.VMEM((2, 2, 64, 1024), F32),
            pltpu.VMEM((256, 1024), BF),
            pltpu.VMEM((8, 16, 8, LANES), F32),
            pltpu.SemaphoreType.DMA((8,)),
        ],
        12,
        10**9,
    )(ladder_tiles, cycle_tiles, partner, total, place_matrix(), same, other, *early, *joined)


def solution(mesh):
    placed = (
        P("pi", "pj", None, "vert"),
        P(None, "vert", None),
        P(),
        P("pj", None, None, "vert"),
        P(),
        P(),
    )
    return jax.shard_map(
        body, mesh=mesh, in_specs=placed, out_specs=P("pi", "pj", None, "vert"), check_vma=False
    )
```

```python
import jax
import jax.numpy as jnp
import numpy as np
from jax import lax
from jax.experimental import pallas as pl
from jax.experimental.pallas import tpu as pltpu
from jax.sharding import PartitionSpec as P

TILE = 64
REACH = 2
BAND = 5
ROWS = 8
LANES = 512
PAIRS = 128
BF = jnp.bfloat16
F32 = jnp.float32
MIB = 1 << 20


def vert_moves(move):
    return [(v, move(v // 4, v % 4)) for v in range(8)]


FLIP = vert_moves(lambda h, y: (1 - h) * 4 + y)
UP = vert_moves(lambda h, y: h * 4 + (y + 1) % 4)
DOWN = vert_moves(lambda h, y: h * 4 + (y + 3) % 4)


def pair_moves(k, dx):
    return [
        ((p * 4 + q) * 8 + v, ((2 * q + ((p % 2) ^ k)) * 4 + p // 2) * 8 + (v ^ (4 * dx)))
        for p in range(8)
        for q in range(4)
        for v in range(8)
    ]


def crosses(device):
    p, q = device // 32, (device // 8) % 4
    return p // 4 != q // 2


def direct_moves(k, dx):
    return [(a, b) for a, b in pair_moves(k, dx) if not crosses(a)]


def relay_moves(k, dx):
    over, along = [], []
    for a, b in pair_moves(k, dx):
        if crosses(a):
            over.append((a, a ^ 16))
            along.append((a ^ 16, b))
    return over, along


def along_moves(block, moves):
    return lax.ppermute(block, ("pi", "pj", "vert"), moves)


def to_transposed(block, k, dx):
    return lax.ppermute(block, ("pi", "pj", "vert"), pair_moves(k, dx))


def along_y(block, dy):
    return lax.ppermute(block, "vert", vert_moves(lambda h, y: h * 4 + (y + dy) % 4))


def peers(sign):
    vert = lax.axis_index("vert")
    h, y = vert // 4, vert % 4
    found = []
    for dx in range(2):
        for dy in range(4):
            there = (h if dx == 0 else 1 - h) * 4 + (y + (dy if sign > 0 else 4 - dy)) % 4
            found.append((dx, dy, pl.multiple_of(there * 128, 128)))
    return found


def crossed():
    return lax.axis_index("pi") // 4 != lax.axis_index("pj") // 2


def split_kernel(same, direct, relayed, first, second, third):
    for dy, ref in enumerate((first, second, third), 1):
        ref[0] = same[dy]
        ref[1] = jnp.where(crossed(), relayed[dy], direct[dy])


def join_kernel(own, first, second, third, same, other):
    for dy, ref in enumerate((own, first, second, third)):
        same[dy] = ref[0]
        other[dy] = ref[1]


def swap_kernel(after, swap_ref):
    del after
    row = lax.broadcasted_iota(jnp.int32, (1024, 128), 0)
    column = lax.broadcasted_iota(jnp.int32, (1024, 128), 1)
    order = ((row >> 3) & 7) * 128 + (row >> 9) * 64 + (row & 7) * 8 + ((row >> 6) & 7) - column
    for c in range(8):
        swap_ref[:, c * 128 : (c + 1) * 128] = jnp.where(order == c * 128, 1.0, 0.0).astype(BF)


def place_matrix():
    row = np.arange(1024)
    v, slot, b, a = row // 128, (row // 64) % 2, (row // 8) % 8, row % 8
    order = jnp.asarray(slot * 512 + b * 64 + v * 8 + a, jnp.int32)
    columns = lax.broadcasted_iota(jnp.int32, (1024, 1024), 1)
    return (order[:, None] == columns).astype(BF)


def second_stage_kernel(before, after, down, up, flip, up_ref, down_ref, side_ref):
    del before, after
    up_ref[:HALF, :] = flip[:HALF, :]
    up_ref[HALF:, :] = up[:HALF, :]
    down_ref[:HALF, :] = flip[:HALF, :]
    down_ref[HALF:, :] = down[HALF:, :]
    side_ref[:HALF, :] = up[HALF:, :]
    side_ref[HALF:, :] = down[HALF:, :]


HALF = 208


def prepare_kernel(*refs):
    inputs, (own_ref, inner_ref, first_ref, last_ref), held = refs[:4], refs[4:8], refs[8:12]
    wide, tall, sems = refs[12:]
    loads = [pltpu.make_async_copy(a, b, sems.at[n]) for n, (a, b) in enumerate(zip(inputs, held))]
    for load in loads:
        load.start()
    ladder_tiles, cycle_tiles, amplitudes, ints = held
    loads[3].wait()
    for n in range(80):
        for t in range(4):
            wide[t, 2 * n : 2 * n + 2, :] = ints[n, :, t * 128 : (t + 1) * 128].astype(F32)
    low = lax.broadcasted_iota(jnp.int32, (80, 128), 1) < TILE
    for t in range(4):
        zero = wide[t, pl.ds(0, 80, stride=2), :]
        one = wide[t, pl.ds(1, 80, stride=2), :]
        tall[pl.ds(2 * t, 80, stride=8), :] = jnp.where(low, zero, pltpu.roll(one, TILE, 1))
        tall[pl.ds(2 * t + 1, 80, stride=8), :] = jnp.where(low, pltpu.roll(zero, TILE, 1), one)
    for b in range(4):
        for w in range(2):
            own_ref[w * HALF + PAIRS : (w + 1) * HALF, b * 128 : (b + 1) * 128] = tall[
                b * 160 + w * 80 : b * 160 + (w + 1) * 80, :
            ].astype(BF)
    row = lax.broadcasted_iota(jnp.int32, (512, 128), 0)
    column = lax.broadcasted_iota(jnp.int32, (512, 128), 1)
    ladder_row = row < 256
    for load in loads[:2]:
        load.wait()
    i = row & 7
    j = jnp.where(ladder_row, (row >> 3) & 15, (row >> 4) & 15)
    which = jnp.where(ladder_row, (row >> 7) & 1, (row >> 3) & 1)
    ladder_0, cycle_0 = ladder_tiles[0, 1], cycle_tiles[0, 1]
    tile = jnp.where(
        ladder_row,
        ladder_0 + which * (ladder_tiles[1, 1] - ladder_0),
        cycle_0 + which * (cycle_tiles[1, 1] - cycle_0),
    )
    wanted = (i * 16 + j) * 8 + tile - column
    pick = jnp.concatenate(
        [jnp.where(wanted == c * 128, 1.0, 0.0).astype(BF) for c in range(8)], axis=1
    )
    loads[2].wait()
    picked = jnp.dot(pick, amplitudes[...], preferred_element_type=F32).astype(BF)
    for w in range(2):
        own_ref[w * HALF : w * HALF + PAIRS, :] = picked[w * PAIRS : (w + 1) * PAIRS]
    inner = picked[256:].reshape(16, 16, LANES)
    inner_ref[...] = inner
    first_ref[...] = inner[:REACH]
    last_ref[...] = inner[16 - REACH :]


def near_pieces(refs):
    own, down, up, flip = refs
    vert = lax.axis_index("vert")
    h, y = vert // 4, vert % 4
    places = [(h, y, own), (h, y + 1, down), (h, y + 3, up), (1 - h, y, flip)]
    return [[(a * 4 + b % 4, ref, w * HALF) for a, b, ref in places] for w in range(2)]


def far_pieces(refs):
    up_2, down_2, side_2, up_3, down_3 = refs
    vert = lax.axis_index("vert")
    h, y = vert // 4, vert % 4
    places = [(1 - h, y + 3), (1 - h, y + 1), (h, y + 2), (1 - h, y + 2)]
    held = [
        [(up_2, 0), (down_2, 0), (up_2, HALF), (down_3, 0)],
        [(side_2, 0), (side_2, HALF), (down_2, HALF), (up_3, 0)],
    ]
    return [
        [(a * 4 + b % 4, ref, first) for (a, b), (ref, first) in zip(places, held[w])]
        for w in range(2)
    ]


def ladder_part(which, pieces, ladder_ints, acc):
    for source, ref, first in pieces:
        start = pl.multiple_of(source * LANES, LANES)
        part = lax.dot_general(
            ref[first : first + PAIRS, :],
            ladder_ints[which, :, pl.ds(start, LANES)],
            (((1,), (1,)), ((), ())),
            preferred_element_type=F32,
        )
        acc = part if acc is None else acc + part
    return acc


def near_kernel(ladder_ints, *refs):
    for which, pieces in enumerate(near_pieces(refs[:4])):
        refs[4][:, which * LANES : (which + 1) * LANES] = ladder_part(
            which, pieces, ladder_ints, None
        )


def main_kernel(ladder_ints, near, before, inner, after, swap, *refs):
    total, same_ref, other_ref, *late_refs, ints, lanes_buf = refs[9:]
    far = far_pieces(refs[4:9])
    for w, pieces in enumerate(near_pieces(refs[:4])):
        for source, ref, first in pieces + far[w]:
            ints[source, w * 80 : (w + 1) * 80, :] = ref[first + PAIRS : first + HALF, :].astype(F32)

    def rows_of(j):
        if j < REACH:
            return before[j]
        if j < REACH + 16:
            return inner[j - REACH]
        return after[j - REACH - 16]

    laid = []
    for j in range(16 + 2 * REACH):
        block = rows_of(j)
        laid.append(
            jnp.concatenate([block[:, a * TILE : (a + 1) * TILE] for a in range(ROWS)], axis=0)
        )
    low = lax.broadcasted_iota(jnp.int32, (8, 128), 1) < TILE
    for j in range(16):
        left = jnp.concatenate([laid[j + o] for o in range(BAND)], axis=1)
        base, lanes = (j % 4) * 40, (j // 4) * 128
        right = jnp.concatenate(
            [
                ints[v, base + o * 8 : base + o * 8 + 8, lanes : lanes + 128]
                for o in range(BAND)
                for v in range(8)
            ],
            axis=0,
        ).astype(BF)
        done = jnp.dot(left, right, preferred_element_type=F32)
        for r in range(2):
            for t in range(4):
                even = done[t * 32 + r * 8 : t * 32 + r * 8 + 8]
                odd = done[t * 32 + 16 + r * 8 : t * 32 + 16 + r * 8 + 8]
                if r == 0:
                    odd = pltpu.roll(odd, TILE, 1)
                else:
                    even = pltpu.roll(even, TILE, 1)
                lane = 1024 + r * LANES + t * 128
                total[j * 8 : j * 8 + 8, lane : lane + 128] = jnp.where(low, even, odd)
    for which in range(2):
        lanes = slice(which * LANES, (which + 1) * LANES)
        total[:, lanes] = ladder_part(which, far[which], ladder_ints, near[:, lanes])
    both = jnp.concatenate([total[:, :1024], total[:, 1024:]], axis=0).astype(BF)
    lanes_buf[...] = jnp.dot(both, swap[...], preferred_element_type=F32).astype(BF)
    parity = lax.axis_index("pi") % 2
    for s in range(2):
        early = pl.ds(pl.multiple_of(s * 128 + parity * 64, 64), 64)
        late = pl.ds(pl.multiple_of(s * 128 + (1 - parity) * 64, 64), 64)
        rows = slice(s * 64, (s + 1) * 64)
        for dx, dy, start in peers(1):
            (same_ref, other_ref)[dx][dy, rows, :] = lanes_buf[early, pl.ds(start, 128)]
            late_refs[dy][dx, rows, :] = lanes_buf[late, pl.ds(start, 128)]


def finish_kernel(ladder_tiles, cycle_tiles, partner, total, place, *refs):
    arrived, (out_ref, mirrored, wide, held, sems) = refs[:8], refs[8:]
    parity = lax.axis_index("pi") % 2
    same, direct, relayed = arrived[:3]
    for dx, dy, start in peers(-1):
        if dy > 0:
            early = arrived[2 + dy][dx]
        elif dx == 0:
            early = same[0]
        else:
            early = jnp.where(crossed(), relayed[0], direct[0])
        wide[:128, pl.ds(start, 128)] = early
        wide[128:, pl.ds(start, 128)] = arrived[6 + dx][dy]
    moved = jnp.dot(wide[...], place[...], preferred_element_type=F32)
    for k in range(2):
        for s in range(2):
            mirrored[s, parity ^ k] = moved[k * 128 + s * 64 : k * 128 + (s + 1) * 64]
    dests = [ladder_tiles[0, 0], ladder_tiles[1, 0], cycle_tiles[0, 0], cycle_tiles[1, 0]]
    tile = lax.broadcasted_iota(jnp.int32, (8, LANES), 0)
    own = [(tile == dest).astype(F32) for dest in dests]
    other = [(tile == partner[dest]).astype(F32) for dest in dests]

    def store(i):
        return pltpu.make_async_copy(held.at[i], out_ref.at[i], sems.at[i])

    def one(i):
        for j in range(16):
            acc = None
            for s in range(4):
                lanes = slice((s % 2) * LANES, (s % 2 + 1) * LANES)
                term = own[s] * total[pl.ds(j * 8 + i, 1), s * LANES : (s + 1) * LANES]
                acc = term if acc is None else acc + term
                acc = acc + other[s] * mirrored[s // 2, j // 8, pl.ds(i * 8 + j % 8, 1), lanes]
            held[i, j] = acc
        store(i).start()

    pl.loop(0, 8)(one)
    pl.loop(0, 8)(lambda i: store(i).wait())


SMEM = pl.BlockSpec(memory_space=pltpu.SMEM)
VMEM = pl.BlockSpec(memory_space=pltpu.VMEM)
HBM = pl.BlockSpec(memory_space=pltpu.HBM)


def call(kernel, ins, outs, out_specs, scratch, limit, flops):
    return pl.pallas_call(
        kernel,
        out_shape=outs,
        in_specs=ins,
        out_specs=out_specs,
        scratch_shapes=scratch,
        compiler_params=pltpu.CompilerParams(vmem_limit_bytes=limit * MIB),
        cost_estimate=pl.CostEstimate(flops=flops, bytes_accessed=4 * MIB, transcendentals=0),
    )


def shape(dims, kind):
    return jax.ShapeDtypeStruct(dims, kind)


def gather(own, before, after):
    down = lax.ppermute(own, "vert", DOWN)
    up = lax.ppermute(own, "vert", UP)
    flip = lax.ppermute(own, "vert", FLIP)
    near = [down, up, flip]
    to_up, to_down, to_side = call(
        second_stage_kernel,
        [HBM] * 2 + [VMEM] * 3,
        [shape((2 * HALF, LANES), BF)] * 3,
        [VMEM] * 3,
        [],
        8,
        10**7,
    )(before, after, *near)
    side_2 = lax.ppermute(to_side, "vert", FLIP)
    up_2 = lax.ppermute(to_up, "vert", UP)
    down_2 = lax.ppermute(to_down, "vert", DOWN)
    up_3 = lax.ppermute(side_2[:HALF], "vert", UP)
    down_3 = lax.ppermute(down_2[:HALF], "vert", DOWN)
    return [own] + near, [up_2, down_2, side_2, up_3, down_3]


def body(amplitudes, ladder_ints, ladder_tiles, cycle_ints, cycle_tiles, partner):
    edge = shape((REACH, 16, LANES), BF)
    own, inner, first, last = call(
        prepare_kernel,
        [HBM] * 4,
        [shape((2 * HALF, LANES), BF), shape((16, 16, LANES), BF), edge, edge],
        [VMEM] * 4,
        [
            pltpu.SMEM((2, 2), jnp.int32),
            pltpu.SMEM((2, 2), jnp.int32),
            pltpu.VMEM((1024, LANES), BF),
            pltpu.VMEM((80, 2, LANES), BF),
            pltpu.VMEM((4, 160, 128), F32),
            pltpu.VMEM((640, 128), F32),
            pltpu.SemaphoreType.DMA((4,)),
        ],
        60,
        10**9,
    )(ladder_tiles, cycle_tiles, amplitudes.reshape(1024, LANES), cycle_ints.reshape(80, 2, LANES))
    before = lax.ppermute(last, "pj", [(q, q + 1) for q in range(3)])
    after = lax.ppermute(first, "pj", [(q + 1, q) for q in range(3)])
    near, far = gather(own, before, after)
    swap = call(
        swap_kernel, [HBM], shape((1024, 1024), BF), VMEM, [], 8, 2 * 10**10
    )(near[1])
    begun = call(
        near_kernel, [VMEM] * 5, shape((PAIRS, 1024), F32), VMEM, [], 8, 10**9
    )(ladder_ints, *near)
    four, two = shape((4, 128, 128), BF), shape((2, 128, 128), BF)
    total, same, other, late_0, late_1, late_2, late_3 = call(
        main_kernel,
        [VMEM] * 15,
        [shape((PAIRS, 2048), F32), four, four, two, two, two, two],
        [VMEM] * 7,
        [pltpu.VMEM((8, 160, LANES), F32), pltpu.VMEM((256, 1024), BF)],
        12,
        2 * 10**9,
    )(ladder_ints, begun, before, inner, after, swap, *near, *far)
    over, along = relay_moves(0, 1)
    relayed = along_moves(along_moves(other, over), along)
    same, other = to_transposed(same, 0, 0), along_moves(other, direct_moves(0, 1))
    late = [along_y(block, dy) for dy, block in ((1, late_1), (2, late_2), (3, late_3))]
    joined = call(join_kernel, [VMEM] * 4, [four] * 2, [VMEM] * 2, [], 4, 10**7)(late_0, *late)
    joined = [to_transposed(block, 1, dx) for dx, block in enumerate(joined)]
    early = call(split_kernel, [VMEM] * 3, [two] * 3, [VMEM] * 3, [], 4, 10**7)(
        same, other, relayed
    )
    early = [along_y(block, dy) for dy, block in enumerate(early, 1)]
    return call(
        finish_kernel,
        [SMEM, SMEM, SMEM] + [VMEM] * 10,
        shape((8, 16, 8, LANES), F32),
        HBM,
        [
            pltpu.VMEM((2, 2, 64, 1024), F32),
            pltpu.VMEM((256, 1024), BF),
            pltpu.VMEM((8, 16, 8, LANES), F32),
            pltpu.SemaphoreType.DMA((8,)),
        ],
        12,
        10**9,
    )(ladder_tiles, cycle_tiles, partner, total, place_matrix(), same, other, relayed, *early, *joined)


def solution(mesh):
    placed = (
        P("pi", "pj", None, "vert"),
        P(None, "vert", None),
        P(),
        P("pj", None, None, "vert"),
        P(),
        P(),
    )
    return jax.shard_map(
        body, mesh=mesh, in_specs=placed, out_specs=P("pi", "pj", None, "vert"), check_vma=False
    )
```

```python
import functools

import jax
import jax.numpy as jnp
import numpy as np
from jax import lax
from jax.experimental import pallas as pl
from jax.experimental.pallas import tpu as pltpu
from jax.sharding import PartitionSpec as P

TILE = 64
REACH = 2
BAND = 5
ROWS = 8
LANES = 512
PAIRS = 128
BF = jnp.bfloat16
F32 = jnp.float32
MIB = 1 << 20


def vert_moves(move):
    return [(v, move(v // 4, v % 4)) for v in range(8)]


FLIP = vert_moves(lambda h, y: (1 - h) * 4 + y)
UP = vert_moves(lambda h, y: h * 4 + (y + 1) % 4)
DOWN = vert_moves(lambda h, y: h * 4 + (y + 3) % 4)


def pair_moves(k, dx):
    return [
        ((p * 4 + q) * 8 + v, ((2 * q + ((p % 2) ^ k)) * 4 + p // 2) * 8 + (v ^ (4 * dx)))
        for p in range(8)
        for q in range(4)
        for v in range(8)
    ]


def to_transposed(block, k, dx):
    return lax.ppermute(block, ("pi", "pj", "vert"), pair_moves(k, dx))


def along_y(block, dy):
    return lax.ppermute(block, "vert", vert_moves(lambda h, y: h * 4 + (y + dy) % 4))


def peers(sign):
    vert = lax.axis_index("vert")
    h, y = vert // 4, vert % 4
    found = []
    for dx in range(2):
        for dy in range(4):
            there = (h if dx == 0 else 1 - h) * 4 + (y + (dy if sign > 0 else 4 - dy)) % 4
            found.append((dx, dy, pl.multiple_of(there * 128, 128)))
    return found


def split_kernel(same, other, first, second, third):
    for dy, ref in enumerate((first, second, third), 1):
        ref[0] = same[dy]
        ref[1] = other[dy]


def join_kernel(own, first, second, third, same, other):
    for dy, ref in enumerate((own, first, second, third)):
        same[dy] = ref[0]
        other[dy] = ref[1]


def swap_kernel(after, swap_ref):
    del after
    row = lax.broadcasted_iota(jnp.int32, (1024, 128), 0)
    column = lax.broadcasted_iota(jnp.int32, (1024, 128), 1)
    order = ((row >> 3) & 7) * 128 + (row >> 9) * 64 + (row & 7) * 8 + ((row >> 6) & 7) - column
    for c in range(8):
        swap_ref[:, c * 128 : (c + 1) * 128] = jnp.where(order == c * 128, 1.0, 0.0).astype(BF)


def place_matrix():
    row = np.arange(1024)
    v, slot, b, a = row // 128, (row // 64) % 2, (row // 8) % 8, row % 8
    order = jnp.asarray(slot * 512 + b * 64 + v * 8 + a, jnp.int32)
    columns = lax.broadcasted_iota(jnp.int32, (1024, 1024), 1)
    return (order[:, None] == columns).astype(BF)


def second_stage_kernel(before, after, down, up, flip, up_ref, down_ref, side_ref):
    del before, after
    up_ref[:HALF, :] = flip[:HALF, :]
    up_ref[HALF:, :] = up[:HALF, :]
    down_ref[:HALF, :] = flip[:HALF, :]
    down_ref[HALF:, :] = down[HALF:, :]
    side_ref[:HALF, :] = up[HALF:, :]
    side_ref[HALF:, :] = down[HALF:, :]


HALF = 208


def prepare_kernel(*refs):
    inputs, (own_ref, inner_ref, first_ref, last_ref), held = refs[:4], refs[4:8], refs[8:12]
    wide, tall, sems = refs[12:]
    loads = [pltpu.make_async_copy(a, b, sems.at[n]) for n, (a, b) in enumerate(zip(inputs, held))]
    for load in loads:
        load.start()
    ladder_tiles, cycle_tiles, amplitudes, ints = held
    loads[3].wait()
    for n in range(80):
        for t in range(4):
            wide[t, 2 * n : 2 * n + 2, :] = ints[n, :, t * 128 : (t + 1) * 128].astype(F32)
    low = lax.broadcasted_iota(jnp.int32, (80, 128), 1) < TILE
    for t in range(4):
        zero = wide[t, pl.ds(0, 80, stride=2), :]
        one = wide[t, pl.ds(1, 80, stride=2), :]
        tall[pl.ds(2 * t, 80, stride=8), :] = jnp.where(low, zero, pltpu.roll(one, TILE, 1))
        tall[pl.ds(2 * t + 1, 80, stride=8), :] = jnp.where(low, pltpu.roll(zero, TILE, 1), one)
    for b in range(4):
        for w in range(2):
            own_ref[w * HALF + PAIRS : (w + 1) * HALF, b * 128 : (b + 1) * 128] = tall[
                b * 160 + w * 80 : b * 160 + (w + 1) * 80, :
            ].astype(BF)
    row = lax.broadcasted_iota(jnp.int32, (512, 128), 0)
    column = lax.broadcasted_iota(jnp.int32, (512, 128), 1)
    ladder_row = row < 256
    for load in loads[:2]:
        load.wait()
    i = row & 7
    j = jnp.where(ladder_row, (row >> 3) & 15, (row >> 4) & 15)
    which = jnp.where(ladder_row, (row >> 7) & 1, (row >> 3) & 1)
    ladder_0, cycle_0 = ladder_tiles[0, 1], cycle_tiles[0, 1]
    tile = jnp.where(
        ladder_row,
        ladder_0 + which * (ladder_tiles[1, 1] - ladder_0),
        cycle_0 + which * (cycle_tiles[1, 1] - cycle_0),
    )
    wanted = (i * 16 + j) * 8 + tile - column
    pick = jnp.concatenate(
        [jnp.where(wanted == c * 128, 1.0, 0.0).astype(BF) for c in range(8)], axis=1
    )
    loads[2].wait()
    picked = jnp.dot(pick, amplitudes[...], preferred_element_type=F32).astype(BF)
    for w in range(2):
        own_ref[w * HALF : w * HALF + PAIRS, :] = picked[w * PAIRS : (w + 1) * PAIRS]
    inner = picked[256:].reshape(16, 16, LANES)
    inner_ref[...] = inner
    first_ref[...] = inner[:REACH]
    last_ref[...] = inner[16 - REACH :]


def near_pieces(refs):
    own, down, up, flip = refs
    vert = lax.axis_index("vert")
    h, y = vert // 4, vert % 4
    places = [(h, y, own), (h, y + 1, down), (h, y + 3, up), (1 - h, y, flip)]
    return [[(a * 4 + b % 4, ref, w * HALF) for a, b, ref in places] for w in range(2)]


def far_pieces(refs):
    up_2, down_2, side_2, up_3, down_3 = refs
    vert = lax.axis_index("vert")
    h, y = vert // 4, vert % 4
    places = [(1 - h, y + 3), (1 - h, y + 1), (h, y + 2), (1 - h, y + 2)]
    held = [
        [(up_2, 0), (down_2, 0), (up_2, HALF), (down_3, 0)],
        [(side_2, 0), (side_2, HALF), (down_2, HALF), (up_3, 0)],
    ]
    return [
        [(a * 4 + b % 4, ref, first) for (a, b), (ref, first) in zip(places, held[w])]
        for w in range(2)
    ]


def ladder_part(which, pieces, ladder_ints, acc):
    for source, ref, first in pieces:
        start = pl.multiple_of(source * LANES, LANES)
        part = lax.dot_general(
            ref[first : first + PAIRS, :],
            ladder_ints[which, :, pl.ds(start, LANES)],
            (((1,), (1,)), ((), ())),
            preferred_element_type=F32,
        )
        acc = part if acc is None else acc + part
    return acc


def near_kernel(ladder_ints, *refs):
    for which, pieces in enumerate(near_pieces(refs[:4])):
        refs[4][:, which * LANES : (which + 1) * LANES] = ladder_part(
            which, pieces, ladder_ints, None
        )


def main_kernel(ladder_ints, near, before, inner, after, swap, *refs):
    total, same_ref, other_ref, *late_refs, ints, lanes_buf = refs[9:]
    far = far_pieces(refs[4:9])
    for w, pieces in enumerate(near_pieces(refs[:4])):
        for source, ref, first in pieces + far[w]:
            ints[source, w * 80 : (w + 1) * 80, :] = ref[first + PAIRS : first + HALF, :].astype(F32)

    def rows_of(j):
        if j < REACH:
            return before[j]
        if j < REACH + 16:
            return inner[j - REACH]
        return after[j - REACH - 16]

    laid = []
    for j in range(16 + 2 * REACH):
        block = rows_of(j)
        laid.append(
            jnp.concatenate([block[:, a * TILE : (a + 1) * TILE] for a in range(ROWS)], axis=0)
        )
    low = lax.broadcasted_iota(jnp.int32, (8, 128), 1) < TILE
    for j in range(16):
        left = jnp.concatenate([laid[j + o] for o in range(BAND)], axis=1)
        base, lanes = (j % 4) * 40, (j // 4) * 128
        right = jnp.concatenate(
            [
                ints[v, base + o * 8 : base + o * 8 + 8, lanes : lanes + 128]
                for o in range(BAND)
                for v in range(8)
            ],
            axis=0,
        ).astype(BF)
        done = jnp.dot(left, right, preferred_element_type=F32)
        for r in range(2):
            for t in range(4):
                even = done[t * 32 + r * 8 : t * 32 + r * 8 + 8]
                odd = done[t * 32 + 16 + r * 8 : t * 32 + 16 + r * 8 + 8]
                if r == 0:
                    odd = pltpu.roll(odd, TILE, 1)
                else:
                    even = pltpu.roll(even, TILE, 1)
                lane = 1024 + r * LANES + t * 128
                total[j * 8 : j * 8 + 8, lane : lane + 128] = jnp.where(low, even, odd)
    for which in range(2):
        lanes = slice(which * LANES, (which + 1) * LANES)
        total[:, lanes] = ladder_part(which, far[which], ladder_ints, near[:, lanes])
    both = jnp.concatenate([total[:, :1024], total[:, 1024:]], axis=0).astype(BF)
    lanes_buf[...] = jnp.dot(both, swap[...], preferred_element_type=F32).astype(BF)
    parity = lax.axis_index("pi") % 2
    for s in range(2):
        early = pl.ds(pl.multiple_of(s * 128 + parity * 64, 64), 64)
        late = pl.ds(pl.multiple_of(s * 128 + (1 - parity) * 64, 64), 64)
        rows = slice(s * 64, (s + 1) * 64)
        for dx, dy, start in peers(1):
            (same_ref, other_ref)[dx][dy, rows, :] = lanes_buf[early, pl.ds(start, 128)]
            late_refs[dy][dx, rows, :] = lanes_buf[late, pl.ds(start, 128)]


def finish_kernel(k, ladder_tiles, cycle_tiles, partner, total, place, *refs):
    arrived, (out_ref, mirrored, wide, held, sems) = refs[:-5], refs[-5:]
    half = (lax.axis_index("pi") % 2) ^ k
    for dx, dy, start in peers(-1):
        if k == 1:
            block = arrived[dx][dy]
        elif dy == 0:
            block = arrived[dx][0]
        else:
            block = arrived[1 + dy][dx]
        wide[:, pl.ds(start, 128)] = block
    mirrored[...] = jnp.dot(wide[...], place[...], preferred_element_type=F32)
    dests = [ladder_tiles[0, 0], ladder_tiles[1, 0], cycle_tiles[0, 0], cycle_tiles[1, 0]]
    tile = lax.broadcasted_iota(jnp.int32, (8, LANES), 0)
    own = [(tile == dest).astype(F32) for dest in dests]
    other = [(tile == partner[dest]).astype(F32) for dest in dests]

    def store(i):
        where = out_ref.at[i, pl.ds(pl.multiple_of(half * 8, 8), 8)]
        return pltpu.make_async_copy(held.at[i], where, sems.at[i])

    def one(i):
        for j in range(8):
            acc = None
            for s in range(4):
                lanes = slice((s % 2) * LANES, (s % 2 + 1) * LANES)
                mine = total[pl.ds(half * 64 + j * 8 + i, 1), s * LANES : (s + 1) * LANES]
                term = own[s] * mine
                acc = term if acc is None else acc + term
                acc = acc + other[s] * mirrored[pl.ds((s // 2) * 64 + i * 8 + j, 1), lanes]
            held[i, j] = acc
        store(i).start()

    pl.loop(0, 8)(one)
    pl.loop(0, 8)(lambda i: store(i).wait())


SMEM = pl.BlockSpec(memory_space=pltpu.SMEM)
VMEM = pl.BlockSpec(memory_space=pltpu.VMEM)
HBM = pl.BlockSpec(memory_space=pltpu.HBM)


def call(kernel, ins, outs, out_specs, scratch, limit, flops, aliases=None):
    return pl.pallas_call(
        kernel,
        out_shape=outs,
        in_specs=ins,
        out_specs=out_specs,
        scratch_shapes=scratch,
        input_output_aliases=aliases or {},
        compiler_params=pltpu.CompilerParams(vmem_limit_bytes=limit * MIB),
        cost_estimate=pl.CostEstimate(flops=flops, bytes_accessed=4 * MIB, transcendentals=0),
    )


def shape(dims, kind):
    return jax.ShapeDtypeStruct(dims, kind)


def gather(own, before, after):
    down = lax.ppermute(own, "vert", DOWN)
    up = lax.ppermute(own, "vert", UP)
    flip = lax.ppermute(own, "vert", FLIP)
    near = [down, up, flip]
    to_up, to_down, to_side = call(
        second_stage_kernel,
        [HBM] * 2 + [VMEM] * 3,
        [shape((2 * HALF, LANES), BF)] * 3,
        [VMEM] * 3,
        [],
        8,
        10**7,
    )(before, after, *near)
    side_2 = lax.ppermute(to_side, "vert", FLIP)
    up_2 = lax.ppermute(to_up, "vert", UP)
    down_2 = lax.ppermute(to_down, "vert", DOWN)
    up_3 = lax.ppermute(side_2[:HALF], "vert", UP)
    down_3 = lax.ppermute(down_2[:HALF], "vert", DOWN)
    return [own] + near, [up_2, down_2, side_2, up_3, down_3]


def body(amplitudes, ladder_ints, ladder_tiles, cycle_ints, cycle_tiles, partner):
    edge = shape((REACH, 16, LANES), BF)
    own, inner, first, last = call(
        prepare_kernel,
        [HBM] * 4,
        [shape((2 * HALF, LANES), BF), shape((16, 16, LANES), BF), edge, edge],
        [VMEM] * 4,
        [
            pltpu.SMEM((2, 2), jnp.int32),
            pltpu.SMEM((2, 2), jnp.int32),
            pltpu.VMEM((1024, LANES), BF),
            pltpu.VMEM((80, 2, LANES), BF),
            pltpu.VMEM((4, 160, 128), F32),
            pltpu.VMEM((640, 128), F32),
            pltpu.SemaphoreType.DMA((4,)),
        ],
        60,
        10**9,
    )(ladder_tiles, cycle_tiles, amplitudes.reshape(1024, LANES), cycle_ints.reshape(80, 2, LANES))
    before = lax.ppermute(last, "pj", [(q, q + 1) for q in range(3)])
    after = lax.ppermute(first, "pj", [(q + 1, q) for q in range(3)])
    near, far = gather(own, before, after)
    swap = call(
        swap_kernel, [HBM], shape((1024, 1024), BF), VMEM, [], 8, 2 * 10**10
    )(near[1])
    begun = call(
        near_kernel, [VMEM] * 5, shape((PAIRS, 1024), F32), VMEM, [], 8, 10**9
    )(ladder_ints, *near)
    four, two = shape((4, 128, 128), BF), shape((2, 128, 128), BF)
    total, same, other, late_0, late_1, late_2, late_3 = call(
        main_kernel,
        [VMEM] * 15,
        [shape((PAIRS, 2048), F32), four, four, two, two, two, two],
        [VMEM] * 7,
        [pltpu.VMEM((8, 160, LANES), F32), pltpu.VMEM((256, 1024), BF)],
        12,
        2 * 10**9,
    )(ladder_ints, begun, before, inner, after, swap, *near, *far)
    same, other = to_transposed(same, 0, 0), to_transposed(other, 0, 1)
    late = [along_y(block, dy) for dy, block in ((1, late_1), (2, late_2), (3, late_3))]
    joined = call(join_kernel, [VMEM] * 4, [four] * 2, [VMEM] * 2, [], 4, 10**7)(late_0, *late)
    joined = [to_transposed(block, 1, dx) for dx, block in enumerate(joined)]
    early = call(split_kernel, [VMEM] * 2, [two] * 3, [VMEM] * 3, [], 4, 10**7)(same, other)
    early = [along_y(block, dy) for dy, block in enumerate(early, 1)]
    scratch = [
        pltpu.VMEM((128, 1024), F32),
        pltpu.VMEM((128, 1024), BF),
        pltpu.VMEM((8, 8, 8, LANES), F32),
        pltpu.SemaphoreType.DMA((8,)),
    ]
    whole = shape((8, 16, 8, LANES), F32)
    common = (ladder_tiles, cycle_tiles, partner, total, place_matrix())
    begun = call(
        functools.partial(finish_kernel, 0),
        [SMEM] * 3 + [VMEM] * 7,
        whole,
        HBM,
        scratch,
        12,
        10**9,
    )(*common, same, other, *early)
    return call(
        functools.partial(finish_kernel, 1),
        [SMEM] * 3 + [VMEM] * 4 + [HBM],
        whole,
        HBM,
        scratch,
        12,
        10**9,
        {7: 0},
    )(*common, *joined, begun)


def solution(mesh):
    placed = (
        P("pi", "pj", None, "vert"),
        P(None, "vert", None),
        P(),
        P("pj", None, None, "vert"),
        P(),
        P(),
    )
    return jax.shard_map(
        body, mesh=mesh, in_specs=placed, out_specs=P("pi", "pj", None, "vert"), check_vma=False
    )
```

```python
import jax
import jax.numpy as jnp
import numpy as np
from jax import lax
from jax.experimental import pallas as pl
from jax.experimental.pallas import tpu as pltpu
from jax.sharding import PartitionSpec as P

TILE = 64
REACH = 2
BAND = 5
ROWS = 8
LANES = 512
PAIRS = 128
BF = jnp.bfloat16
F32 = jnp.float32
MIB = 1 << 20


def vert_moves(move):
    return [(v, move(v // 4, v % 4)) for v in range(8)]


FLIP = vert_moves(lambda h, y: (1 - h) * 4 + y)
UP = vert_moves(lambda h, y: h * 4 + (y + 1) % 4)
DOWN = vert_moves(lambda h, y: h * 4 + (y + 3) % 4)


def pair_moves(k, dx):
    return [
        ((p * 4 + q) * 8 + v, ((2 * q + ((p % 2) ^ k)) * 4 + p // 2) * 8 + (v ^ (4 * dx)))
        for p in range(8)
        for q in range(4)
        for v in range(8)
    ]


def to_transposed(block, k, dx):
    return lax.ppermute(block, ("pi", "pj", "vert"), pair_moves(k, dx))


def along_y(block, dy):
    return lax.ppermute(block, "vert", vert_moves(lambda h, y: h * 4 + (y + dy) % 4))


def peers(sign):
    vert = lax.axis_index("vert")
    h, y = vert // 4, vert % 4
    found = []
    for dx in range(2):
        for dy in range(4):
            there = (h if dx == 0 else 1 - h) * 4 + (y + (dy if sign > 0 else 4 - dy)) % 4
            found.append((dx, dy, pl.multiple_of(there * 128, 128)))
    return found


def split_kernel(same, other, first, second, third):
    for dy, ref in enumerate((first, second, third), 1):
        ref[0] = same[dy]
        ref[1] = other[dy]


def join_kernel(own, first, second, third, same, other):
    for dy, ref in enumerate((own, first, second, third)):
        same[dy] = ref[0]
        other[dy] = ref[1]


def swap_kernel(after, swap_ref):
    del after
    row = lax.broadcasted_iota(jnp.int32, (1024, 128), 0)
    column = lax.broadcasted_iota(jnp.int32, (1024, 128), 1)
    order = ((row >> 3) & 7) * 128 + (row >> 9) * 64 + (row & 7) * 8 + ((row >> 6) & 7) - column
    for c in range(8):
        swap_ref[:, c * 128 : (c + 1) * 128] = jnp.where(order == c * 128, 1.0, 0.0).astype(BF)


def place_matrix():
    row = np.arange(1024)
    v, slot, b, a = row // 128, (row // 64) % 2, (row // 8) % 8, row % 8
    order = jnp.asarray(slot * 512 + b * 64 + v * 8 + a, jnp.int32)
    columns = lax.broadcasted_iota(jnp.int32, (1024, 1024), 1)
    return (order[:, None] == columns).astype(BF)


def second_stage_kernel(before, after, down, up, flip, up_ref, down_ref, side_ref):
    del before, after
    up_ref[:HALF, :] = flip[:HALF, :]
    up_ref[HALF:, :] = up[:HALF, :]
    down_ref[:HALF, :] = flip[:HALF, :]
    down_ref[HALF:, :] = down[HALF:, :]
    side_ref[:HALF, :] = up[HALF:, :]
    side_ref[HALF:, :] = down[HALF:, :]


HALF = 208


def prepare_kernel(*refs):
    inputs, (own_ref, inner_ref, first_ref, last_ref), held = refs[:4], refs[4:8], refs[8:12]
    wide, tall, sems = refs[12:]
    loads = [pltpu.make_async_copy(a, b, sems.at[n]) for n, (a, b) in enumerate(zip(inputs, held))]
    for load in loads:
        load.start()
    ladder_tiles, cycle_tiles, amplitudes, ints = held
    loads[3].wait()
    for n in range(80):
        for t in range(4):
            wide[t, 2 * n : 2 * n + 2, :] = ints[n, :, t * 128 : (t + 1) * 128].astype(F32)
    low = lax.broadcasted_iota(jnp.int32, (80, 128), 1) < TILE
    for t in range(4):
        zero = wide[t, pl.ds(0, 80, stride=2), :]
        one = wide[t, pl.ds(1, 80, stride=2), :]
        tall[pl.ds(2 * t, 80, stride=8), :] = jnp.where(low, zero, pltpu.roll(one, TILE, 1))
        tall[pl.ds(2 * t + 1, 80, stride=8), :] = jnp.where(low, pltpu.roll(zero, TILE, 1), one)
    for b in range(4):
        for w in range(2):
            own_ref[w * HALF + PAIRS : (w + 1) * HALF, b * 128 : (b + 1) * 128] = tall[
                b * 160 + w * 80 : b * 160 + (w + 1) * 80, :
            ].astype(BF)
    row = lax.broadcasted_iota(jnp.int32, (512, 128), 0)
    column = lax.broadcasted_iota(jnp.int32, (512, 128), 1)
    ladder_row = row < 256
    for load in loads[:2]:
        load.wait()
    i = row & 7
    j = jnp.where(ladder_row, (row >> 3) & 15, (row >> 4) & 15)
    which = jnp.where(ladder_row, (row >> 7) & 1, (row >> 3) & 1)
    ladder_0, cycle_0 = ladder_tiles[0, 1], cycle_tiles[0, 1]
    tile = jnp.where(
        ladder_row,
        ladder_0 + which * (ladder_tiles[1, 1] - ladder_0),
        cycle_0 + which * (cycle_tiles[1, 1] - cycle_0),
    )
    wanted = (i * 16 + j) * 8 + tile - column
    pick = jnp.concatenate(
        [jnp.where(wanted == c * 128, 1.0, 0.0).astype(BF) for c in range(8)], axis=1
    )
    loads[2].wait()
    picked = jnp.dot(pick, amplitudes[...], preferred_element_type=F32).astype(BF)
    for w in range(2):
        own_ref[w * HALF : w * HALF + PAIRS, :] = picked[w * PAIRS : (w + 1) * PAIRS]
    inner = picked[256:].reshape(16, 16, LANES)
    inner_ref[...] = inner
    first_ref[...] = inner[:REACH]
    last_ref[...] = inner[16 - REACH :]


def near_pieces(refs):
    own, down, up, flip = refs
    vert = lax.axis_index("vert")
    h, y = vert // 4, vert % 4
    places = [(h, y, own), (h, y + 1, down), (h, y + 3, up), (1 - h, y, flip)]
    return [[(a * 4 + b % 4, ref, w * HALF) for a, b, ref in places] for w in range(2)]


def far_pieces(refs):
    up_2, down_2, side_2, up_3, down_3 = refs
    vert = lax.axis_index("vert")
    h, y = vert // 4, vert % 4
    places = [(1 - h, y + 3), (1 - h, y + 1), (h, y + 2), (1 - h, y + 2)]
    held = [
        [(up_2, 0), (down_2, 0), (up_2, HALF), (down_3, 0)],
        [(side_2, 0), (side_2, HALF), (down_2, HALF), (up_3, 0)],
    ]
    return [
        [(a * 4 + b % 4, ref, first) for (a, b), (ref, first) in zip(places, held[w])]
        for w in range(2)
    ]


def ladder_part(which, pieces, ladder_ints, acc):
    for source, ref, first in pieces:
        start = pl.multiple_of(source * LANES, LANES)
        part = lax.dot_general(
            ref[first : first + PAIRS, :],
            ladder_ints[which, :, pl.ds(start, LANES)],
            (((1,), (1,)), ((), ())),
            preferred_element_type=F32,
        )
        acc = part if acc is None else acc + part
    return acc


def near_kernel(ladder_ints, *refs):
    far = far_pieces(list(refs[4:7]) + [None, None])
    for which, pieces in enumerate(near_pieces(refs[:4])):
        refs[7][:, which * LANES : (which + 1) * LANES] = ladder_part(
            which, pieces + far[which][:3], ladder_ints, None
        )


def main_kernel(ladder_ints, near, before, inner, after, swap, *refs):
    total, same_ref, other_ref, *late_refs, ints, lanes_buf = refs[9:]
    far = far_pieces(refs[4:9])
    for w, pieces in enumerate(near_pieces(refs[:4])):
        for source, ref, first in pieces + far[w]:
            ints[source, w * 80 : (w + 1) * 80, :] = ref[first + PAIRS : first + HALF, :].astype(F32)

    def rows_of(j):
        if j < REACH:
            return before[j]
        if j < REACH + 16:
            return inner[j - REACH]
        return after[j - REACH - 16]

    laid = []
    for j in range(16 + 2 * REACH):
        block = rows_of(j)
        laid.append(
            jnp.concatenate([block[:, a * TILE : (a + 1) * TILE] for a in range(ROWS)], axis=0)
        )
    low = lax.broadcasted_iota(jnp.int32, (8, 128), 1) < TILE
    for j in range(16):
        left = jnp.concatenate([laid[j + o] for o in range(BAND)], axis=1)
        base, lanes = (j % 4) * 40, (j // 4) * 128
        right = jnp.concatenate(
            [
                ints[v, base + o * 8 : base + o * 8 + 8, lanes : lanes + 128]
                for o in range(BAND)
                for v in range(8)
            ],
            axis=0,
        ).astype(BF)
        done = jnp.dot(left, right, preferred_element_type=F32)
        for r in range(2):
            for t in range(4):
                even = done[t * 32 + r * 8 : t * 32 + r * 8 + 8]
                odd = done[t * 32 + 16 + r * 8 : t * 32 + 16 + r * 8 + 8]
                if r == 0:
                    odd = pltpu.roll(odd, TILE, 1)
                else:
                    even = pltpu.roll(even, TILE, 1)
                lane = 1024 + r * LANES + t * 128
                total[j * 8 : j * 8 + 8, lane : lane + 128] = jnp.where(low, even, odd)
    for which in range(2):
        lanes = slice(which * LANES, (which + 1) * LANES)
        total[:, lanes] = ladder_part(which, far[which][3:], ladder_ints, near[:, lanes])
    both = jnp.concatenate([total[:, :1024], total[:, 1024:]], axis=0).astype(BF)
    lanes_buf[...] = jnp.dot(both, swap[...], preferred_element_type=F32).astype(BF)
    parity = lax.axis_index("pi") % 2
    for s in range(2):
        early = pl.ds(pl.multiple_of(s * 128 + parity * 64, 64), 64)
        late = pl.ds(pl.multiple_of(s * 128 + (1 - parity) * 64, 64), 64)
        rows = slice(s * 64, (s + 1) * 64)
        for dx, dy, start in peers(1):
            (same_ref, other_ref)[dx][dy, rows, :] = lanes_buf[early, pl.ds(start, 128)]
            late_refs[dy][dx, rows, :] = lanes_buf[late, pl.ds(start, 128)]


def finish_kernel(ladder_tiles, cycle_tiles, partner, total, place, *refs):
    arrived, (out_ref, mirrored, wide, held, sems) = refs[:7], refs[7:]
    parity = lax.axis_index("pi") % 2
    for dx, dy, start in peers(-1):
        early = arrived[dx][0] if dy == 0 else arrived[1 + dy][dx]
        wide[:128, pl.ds(start, 128)] = early
        wide[128:, pl.ds(start, 128)] = arrived[5 + dx][dy]
    moved = jnp.dot(wide[...], place[...], preferred_element_type=F32)
    for k in range(2):
        for s in range(2):
            mirrored[s, parity ^ k] = moved[k * 128 + s * 64 : k * 128 + (s + 1) * 64]
    dests = [ladder_tiles[0, 0], ladder_tiles[1, 0], cycle_tiles[0, 0], cycle_tiles[1, 0]]
    tile = lax.broadcasted_iota(jnp.int32, (8, LANES), 0)
    own = [(tile == dest).astype(F32) for dest in dests]
    other = [(tile == partner[dest]).astype(F32) for dest in dests]

    def store(i):
        return pltpu.make_async_copy(held.at[i], out_ref.at[i], sems.at[i])

    def one(i):
        for j in range(16):
            acc = None
            for s in range(4):
                lanes = slice((s % 2) * LANES, (s % 2 + 1) * LANES)
                term = own[s] * total[pl.ds(j * 8 + i, 1), s * LANES : (s + 1) * LANES]
                acc = term if acc is None else acc + term
                acc = acc + other[s] * mirrored[s // 2, j // 8, pl.ds(i * 8 + j % 8, 1), lanes]
            held[i, j] = acc
        store(i).start()

    pl.loop(0, 8)(one)
    pl.loop(0, 8)(lambda i: store(i).wait())


SMEM = pl.BlockSpec(memory_space=pltpu.SMEM)
VMEM = pl.BlockSpec(memory_space=pltpu.VMEM)
HBM = pl.BlockSpec(memory_space=pltpu.HBM)


def call(kernel, ins, outs, out_specs, scratch, limit, flops):
    return pl.pallas_call(
        kernel,
        out_shape=outs,
        in_specs=ins,
        out_specs=out_specs,
        scratch_shapes=scratch,
        compiler_params=pltpu.CompilerParams(vmem_limit_bytes=limit * MIB),
        cost_estimate=pl.CostEstimate(flops=flops, bytes_accessed=4 * MIB, transcendentals=0),
    )


def shape(dims, kind):
    return jax.ShapeDtypeStruct(dims, kind)


def gather(own, before, after):
    down = lax.ppermute(own, "vert", DOWN)
    up = lax.ppermute(own, "vert", UP)
    flip = lax.ppermute(own, "vert", FLIP)
    near = [down, up, flip]
    to_up, to_down, to_side = call(
        second_stage_kernel,
        [HBM] * 2 + [VMEM] * 3,
        [shape((2 * HALF, LANES), BF)] * 3,
        [VMEM] * 3,
        [],
        8,
        10**7,
    )(before, after, *near)
    side_2 = lax.ppermute(to_side, "vert", FLIP)
    up_2 = lax.ppermute(to_up, "vert", UP)
    down_2 = lax.ppermute(to_down, "vert", DOWN)
    up_3 = lax.ppermute(side_2[:HALF], "vert", UP)
    down_3 = lax.ppermute(down_2[:HALF], "vert", DOWN)
    return [own] + near, [up_2, down_2, side_2, up_3, down_3]


def body(amplitudes, ladder_ints, ladder_tiles, cycle_ints, cycle_tiles, partner):
    edge = shape((REACH, 16, LANES), BF)
    own, inner, first, last = call(
        prepare_kernel,
        [HBM] * 4,
        [shape((2 * HALF, LANES), BF), shape((16, 16, LANES), BF), edge, edge],
        [VMEM] * 4,
        [
            pltpu.SMEM((2, 2), jnp.int32),
            pltpu.SMEM((2, 2), jnp.int32),
            pltpu.VMEM((1024, LANES), BF),
            pltpu.VMEM((80, 2, LANES), BF),
            pltpu.VMEM((4, 160, 128), F32),
            pltpu.VMEM((640, 128), F32),
            pltpu.SemaphoreType.DMA((4,)),
        ],
        60,
        10**9,
    )(ladder_tiles, cycle_tiles, amplitudes.reshape(1024, LANES), cycle_ints.reshape(80, 2, LANES))
    before = lax.ppermute(last, "pj", [(q, q + 1) for q in range(3)])
    after = lax.ppermute(first, "pj", [(q + 1, q) for q in range(3)])
    near, far = gather(own, before, after)
    swap = call(
        swap_kernel, [HBM], shape((1024, 1024), BF), VMEM, [], 8, 2 * 10**10
    )(near[1])
    begun = call(
        near_kernel, [VMEM] * 8, shape((PAIRS, 1024), F32), VMEM, [], 8, 10**9
    )(ladder_ints, *near, *far[:3])
    four, two = shape((4, 128, 128), BF), shape((2, 128, 128), BF)
    total, same, other, late_0, late_1, late_2, late_3 = call(
        main_kernel,
        [VMEM] * 15,
        [shape((PAIRS, 2048), F32), four, four, two, two, two, two],
        [VMEM] * 7,
        [pltpu.VMEM((8, 160, LANES), F32), pltpu.VMEM((256, 1024), BF)],
        12,
        2 * 10**9,
    )(ladder_ints, begun, before, inner, after, swap, *near, *far)
    same, other = to_transposed(same, 0, 0), to_transposed(other, 0, 1)
    late = [along_y(block, dy) for dy, block in ((1, late_1), (2, late_2), (3, late_3))]
    joined = call(join_kernel, [VMEM] * 4, [four] * 2, [VMEM] * 2, [], 4, 10**7)(late_0, *late)
    joined = [to_transposed(block, 1, dx) for dx, block in enumerate(joined)]
    early = call(split_kernel, [VMEM] * 2, [two] * 3, [VMEM] * 3, [], 4, 10**7)(same, other)
    early = [along_y(block, dy) for dy, block in enumerate(early, 1)]
    return call(
        finish_kernel,
        [SMEM, SMEM, SMEM] + [VMEM] * 9,
        shape((8, 16, 8, LANES), F32),
        HBM,
        [
            pltpu.VMEM((2, 2, 64, 1024), F32),
            pltpu.VMEM((256, 1024), BF),
            pltpu.VMEM((8, 16, 8, LANES), F32),
            pltpu.SemaphoreType.DMA((8,)),
        ],
        12,
        10**9,
    )(ladder_tiles, cycle_tiles, partner, total, place_matrix(), same, other, *early, *joined)


def solution(mesh):
    placed = (
        P("pi", "pj", None, "vert"),
        P(None, "vert", None),
        P(),
        P("pj", None, None, "vert"),
        P(),
        P(),
    )
    return jax.shard_map(
        body, mesh=mesh, in_specs=placed, out_specs=P("pi", "pj", None, "vert"), check_vma=False
    )
```

```python
import jax
import jax.numpy as jnp
import numpy as np
from jax import lax
from jax.experimental import pallas as pl
from jax.experimental.pallas import tpu as pltpu
from jax.sharding import PartitionSpec as P

TILE = 64
REACH = 2
BAND = 5
ROWS = 8
LANES = 512
PAIRS = 128
BF = jnp.bfloat16
F32 = jnp.float32
MIB = 1 << 20


def vert_moves(move):
    return [(v, move(v // 4, v % 4)) for v in range(8)]


FLIP = vert_moves(lambda h, y: (1 - h) * 4 + y)
UP = vert_moves(lambda h, y: h * 4 + (y + 1) % 4)
DOWN = vert_moves(lambda h, y: h * 4 + (y + 3) % 4)


def pair_moves(k, dx):
    return [
        ((p * 4 + q) * 8 + v, ((2 * q + ((p % 2) ^ k)) * 4 + p // 2) * 8 + (v ^ (4 * dx)))
        for p in range(8)
        for q in range(4)
        for v in range(8)
    ]


def to_transposed(block, k, dx):
    return lax.ppermute(block, ("pi", "pj", "vert"), pair_moves(k, dx))


def along_y(block, dy):
    return lax.ppermute(block, "vert", vert_moves(lambda h, y: h * 4 + (y + dy) % 4))


def peers(sign):
    vert = lax.axis_index("vert")
    h, y = vert // 4, vert % 4
    found = []
    for dx in range(2):
        for dy in range(4):
            there = (h if dx == 0 else 1 - h) * 4 + (y + (dy if sign > 0 else 4 - dy)) % 4
            found.append((dx, dy, pl.multiple_of(there * 128, 128)))
    return found


def split_kernel(same, other, first, second, third):
    for dy, ref in enumerate((first, second, third), 1):
        ref[0] = same[dy]
        ref[1] = other[dy]


def join_kernel(own, first, second, third, same, other):
    for dy, ref in enumerate((own, first, second, third)):
        same[dy] = ref[0]
        other[dy] = ref[1]


def swap_kernel(after, swap_ref):
    del after
    row = lax.broadcasted_iota(jnp.int32, (1024, 128), 0)
    column = lax.broadcasted_iota(jnp.int32, (1024, 128), 1)
    order = ((row >> 3) & 7) * 128 + (row >> 9) * 64 + (row & 7) * 8 + ((row >> 6) & 7) - column
    for c in range(8):
        swap_ref[:, c * 128 : (c + 1) * 128] = jnp.where(order == c * 128, 1.0, 0.0).astype(BF)


def place_matrix():
    row = np.arange(1024)
    v, slot, b, a = row // 128, (row // 64) % 2, (row // 8) % 8, row % 8
    order = jnp.asarray(slot * 512 + b * 64 + v * 8 + a, jnp.int32)
    columns = lax.broadcasted_iota(jnp.int32, (1024, 1024), 1)
    return (order[:, None] == columns).astype(BF)


def second_stage_kernel(before, after, down, up, flip, up_ref, down_ref, side_ref):
    del before, after
    up_ref[:HALF, :] = flip[:HALF, :]
    up_ref[HALF:, :] = up[:HALF, :]
    down_ref[:HALF, :] = flip[:HALF, :]
    down_ref[HALF:, :] = down[HALF:, :]
    side_ref[:HALF, :] = up[HALF:, :]
    side_ref[HALF:, :] = down[HALF:, :]


HALF = 208


def prepare_kernel(*refs):
    inputs, (own_ref, inner_ref, first_ref, last_ref), held = refs[:4], refs[4:8], refs[8:12]
    wide, tall, sems = refs[12:]
    loads = [pltpu.make_async_copy(a, b, sems.at[n]) for n, (a, b) in enumerate(zip(inputs, held))]
    for load in loads:
        load.start()
    ladder_tiles, cycle_tiles, amplitudes, ints = held
    loads[3].wait()
    for n in range(80):
        for t in range(4):
            wide[t, 2 * n : 2 * n + 2, :] = ints[n, :, t * 128 : (t + 1) * 128].astype(F32)
    low = lax.broadcasted_iota(jnp.int32, (80, 128), 1) < TILE
    for t in range(4):
        zero = wide[t, pl.ds(0, 80, stride=2), :]
        one = wide[t, pl.ds(1, 80, stride=2), :]
        tall[pl.ds(2 * t, 80, stride=8), :] = jnp.where(low, zero, pltpu.roll(one, TILE, 1))
        tall[pl.ds(2 * t + 1, 80, stride=8), :] = jnp.where(low, pltpu.roll(zero, TILE, 1), one)
    for b in range(4):
        for w in range(2):
            own_ref[w * HALF + PAIRS : (w + 1) * HALF, b * 128 : (b + 1) * 128] = tall[
                b * 160 + w * 80 : b * 160 + (w + 1) * 80, :
            ].astype(BF)
    row = lax.broadcasted_iota(jnp.int32, (512, 128), 0)
    column = lax.broadcasted_iota(jnp.int32, (512, 128), 1)
    ladder_row = row < 256
    for load in loads[:2]:
        load.wait()
    i = row & 7
    j = jnp.where(ladder_row, (row >> 3) & 15, (row >> 4) & 15)
    which = jnp.where(ladder_row, (row >> 7) & 1, (row >> 3) & 1)
    ladder_0, cycle_0 = ladder_tiles[0, 1], cycle_tiles[0, 1]
    tile = jnp.where(
        ladder_row,
        ladder_0 + which * (ladder_tiles[1, 1] - ladder_0),
        cycle_0 + which * (cycle_tiles[1, 1] - cycle_0),
    )
    wanted = (i * 16 + j) * 8 + tile - column
    pick = jnp.concatenate(
        [jnp.where(wanted == c * 128, 1.0, 0.0).astype(BF) for c in range(8)], axis=1
    )
    loads[2].wait()
    picked = jnp.dot(pick, amplitudes[...], preferred_element_type=F32).astype(BF)
    for w in range(2):
        own_ref[w * HALF : w * HALF + PAIRS, :] = picked[w * PAIRS : (w + 1) * PAIRS]
    inner = picked[256:].reshape(16, 16, LANES)
    inner_ref[...] = inner
    first_ref[...] = inner[:REACH]
    last_ref[...] = inner[16 - REACH :]


def near_pieces(refs):
    own, down, up, flip = refs
    vert = lax.axis_index("vert")
    h, y = vert // 4, vert % 4
    places = [(h, y, own), (h, y + 1, down), (h, y + 3, up), (1 - h, y, flip)]
    return [[(a * 4 + b % 4, ref, w * HALF) for a, b, ref in places] for w in range(2)]


def far_pieces(refs):
    up_2, down_2, side_2, up_3, down_3 = refs
    vert = lax.axis_index("vert")
    h, y = vert // 4, vert % 4
    places = [(1 - h, y + 3), (1 - h, y + 1), (h, y + 2), (1 - h, y + 2)]
    held = [
        [(up_2, 0), (down_2, 0), (up_2, HALF), (down_3, 0)],
        [(side_2, 0), (side_2, HALF), (down_2, HALF), (up_3, 0)],
    ]
    return [
        [(a * 4 + b % 4, ref, first) for (a, b), (ref, first) in zip(places, held[w])]
        for w in range(2)
    ]


def ladder_part(which, pieces, ladder_ints, acc):
    for source, ref, first in pieces:
        start = pl.multiple_of(source * LANES, LANES)
        part = lax.dot_general(
            ref[first : first + PAIRS, :],
            ladder_ints[which, :, pl.ds(start, LANES)],
            (((1,), (1,)), ((), ())),
            preferred_element_type=F32,
        )
        acc = part if acc is None else acc + part
    return acc


def near_kernel(ladder_ints, before, inner, after, *refs):
    def rows_of(j):
        if j < REACH:
            return before[j]
        if j < REACH + 16:
            return inner[j - REACH]
        return after[j - REACH - 16]

    for j in range(16 + 2 * REACH):
        block = rows_of(j)
        refs[8][j] = jnp.concatenate(
            [block[:, a * TILE : (a + 1) * TILE] for a in range(ROWS)], axis=0
        )
    far = far_pieces(list(refs[4:7]) + [None, None])
    for which, pieces in enumerate(near_pieces(refs[:4])):
        refs[7][:, which * LANES : (which + 1) * LANES] = ladder_part(
            which, pieces + far[which][:3], ladder_ints, None
        )


def main_kernel(ladder_ints, near, laid, swap, *refs):
    total, same_ref, other_ref, *late_refs, ints, lanes_buf = refs[9:]
    far = far_pieces(refs[4:9])
    for w, pieces in enumerate(near_pieces(refs[:4])):
        for source, ref, first in pieces + far[w]:
            ints[source, w * 80 : (w + 1) * 80, :] = ref[first + PAIRS : first + HALF, :].astype(F32)

    low = lax.broadcasted_iota(jnp.int32, (8, 128), 1) < TILE
    for j in range(16):
        left = jnp.concatenate([laid[j + o] for o in range(BAND)], axis=1)
        base, lanes = (j % 4) * 40, (j // 4) * 128
        right = jnp.concatenate(
            [
                ints[v, base + o * 8 : base + o * 8 + 8, lanes : lanes + 128]
                for o in range(BAND)
                for v in range(8)
            ],
            axis=0,
        ).astype(BF)
        done = jnp.dot(left, right, preferred_element_type=F32)
        for r in range(2):
            for t in range(4):
                even = done[t * 32 + r * 8 : t * 32 + r * 8 + 8]
                odd = done[t * 32 + 16 + r * 8 : t * 32 + 16 + r * 8 + 8]
                if r == 0:
                    odd = pltpu.roll(odd, TILE, 1)
                else:
                    even = pltpu.roll(even, TILE, 1)
                lane = 1024 + r * LANES + t * 128
                total[j * 8 : j * 8 + 8, lane : lane + 128] = jnp.where(low, even, odd)
    for which in range(2):
        lanes = slice(which * LANES, (which + 1) * LANES)
        total[:, lanes] = ladder_part(which, far[which][3:], ladder_ints, near[:, lanes])
    both = jnp.concatenate([total[:, :1024], total[:, 1024:]], axis=0).astype(BF)
    lanes_buf[...] = jnp.dot(both, swap[...], preferred_element_type=F32).astype(BF)
    parity = lax.axis_index("pi") % 2
    for s in range(2):
        early = pl.ds(pl.multiple_of(s * 128 + parity * 64, 64), 64)
        late = pl.ds(pl.multiple_of(s * 128 + (1 - parity) * 64, 64), 64)
        rows = slice(s * 64, (s + 1) * 64)
        for dx, dy, start in peers(1):
            (same_ref, other_ref)[dx][dy, rows, :] = lanes_buf[early, pl.ds(start, 128)]
            late_refs[dy][dx, rows, :] = lanes_buf[late, pl.ds(start, 128)]


def finish_kernel(ladder_tiles, cycle_tiles, partner, total, place, *refs):
    arrived, (out_ref, mirrored, wide, held, sems) = refs[:7], refs[7:]
    parity = lax.axis_index("pi") % 2
    for dx, dy, start in peers(-1):
        early = arrived[dx][0] if dy == 0 else arrived[1 + dy][dx]
        wide[:128, pl.ds(start, 128)] = early
        wide[128:, pl.ds(start, 128)] = arrived[5 + dx][dy]
    moved = jnp.dot(wide[...], place[...], preferred_element_type=F32)
    for k in range(2):
        for s in range(2):
            mirrored[s, parity ^ k] = moved[k * 128 + s * 64 : k * 128 + (s + 1) * 64]
    dests = [ladder_tiles[0, 0], ladder_tiles[1, 0], cycle_tiles[0, 0], cycle_tiles[1, 0]]
    tile = lax.broadcasted_iota(jnp.int32, (8, LANES), 0)
    own = [(tile == dest).astype(F32) for dest in dests]
    other = [(tile == partner[dest]).astype(F32) for dest in dests]

    def store(i):
        return pltpu.make_async_copy(held.at[i], out_ref.at[i], sems.at[i])

    def one(i):
        for j in range(16):
            acc = None
            for s in range(4):
                lanes = slice((s % 2) * LANES, (s % 2 + 1) * LANES)
                term = own[s] * total[pl.ds(j * 8 + i, 1), s * LANES : (s + 1) * LANES]
                acc = term if acc is None else acc + term
                acc = acc + other[s] * mirrored[s // 2, j // 8, pl.ds(i * 8 + j % 8, 1), lanes]
            held[i, j] = acc
        store(i).start()

    pl.loop(0, 8)(one)
    pl.loop(0, 8)(lambda i: store(i).wait())


SMEM = pl.BlockSpec(memory_space=pltpu.SMEM)
VMEM = pl.BlockSpec(memory_space=pltpu.VMEM)
HBM = pl.BlockSpec(memory_space=pltpu.HBM)


def call(kernel, ins, outs, out_specs, scratch, limit, flops):
    return pl.pallas_call(
        kernel,
        out_shape=outs,
        in_specs=ins,
        out_specs=out_specs,
        scratch_shapes=scratch,
        compiler_params=pltpu.CompilerParams(vmem_limit_bytes=limit * MIB),
        cost_estimate=pl.CostEstimate(flops=flops, bytes_accessed=4 * MIB, transcendentals=0),
    )


def shape(dims, kind):
    return jax.ShapeDtypeStruct(dims, kind)


def gather(own, before, after):
    down = lax.ppermute(own, "vert", DOWN)
    up = lax.ppermute(own, "vert", UP)
    flip = lax.ppermute(own, "vert", FLIP)
    near = [down, up, flip]
    to_up, to_down, to_side = call(
        second_stage_kernel,
        [HBM] * 2 + [VMEM] * 3,
        [shape((2 * HALF, LANES), BF)] * 3,
        [VMEM] * 3,
        [],
        8,
        10**7,
    )(before, after, *near)
    side_2 = lax.ppermute(to_side, "vert", FLIP)
    up_2 = lax.ppermute(to_up, "vert", UP)
    down_2 = lax.ppermute(to_down, "vert", DOWN)
    up_3 = lax.ppermute(side_2[:HALF], "vert", UP)
    down_3 = lax.ppermute(down_2[:HALF], "vert", DOWN)
    return [own] + near, [up_2, down_2, side_2, up_3, down_3]


def body(amplitudes, ladder_ints, ladder_tiles, cycle_ints, cycle_tiles, partner):
    edge = shape((REACH, 16, LANES), BF)
    own, inner, first, last = call(
        prepare_kernel,
        [HBM] * 4,
        [shape((2 * HALF, LANES), BF), shape((16, 16, LANES), BF), edge, edge],
        [VMEM] * 4,
        [
            pltpu.SMEM((2, 2), jnp.int32),
            pltpu.SMEM((2, 2), jnp.int32),
            pltpu.VMEM((1024, LANES), BF),
            pltpu.VMEM((80, 2, LANES), BF),
            pltpu.VMEM((4, 160, 128), F32),
            pltpu.VMEM((640, 128), F32),
            pltpu.SemaphoreType.DMA((4,)),
        ],
        60,
        10**9,
    )(ladder_tiles, cycle_tiles, amplitudes.reshape(1024, LANES), cycle_ints.reshape(80, 2, LANES))
    before = lax.ppermute(last, "pj", [(q, q + 1) for q in range(3)])
    after = lax.ppermute(first, "pj", [(q + 1, q) for q in range(3)])
    near, far = gather(own, before, after)
    swap = call(
        swap_kernel, [HBM], shape((1024, 1024), BF), VMEM, [], 8, 2 * 10**10
    )(near[1])
    begun, laid = call(
        near_kernel,
        [VMEM] * 11,
        [shape((PAIRS, 1024), F32), shape((16 + 2 * REACH, PAIRS, TILE), BF)],
        [VMEM] * 2,
        [],
        8,
        10**9,
    )(ladder_ints, before, inner, after, *near, *far[:3])
    four, two = shape((4, 128, 128), BF), shape((2, 128, 128), BF)
    total, same, other, late_0, late_1, late_2, late_3 = call(
        main_kernel,
        [VMEM] * 13,
        [shape((PAIRS, 2048), F32), four, four, two, two, two, two],
        [VMEM] * 7,
        [pltpu.VMEM((8, 160, LANES), F32), pltpu.VMEM((256, 1024), BF)],
        12,
        2 * 10**9,
    )(ladder_ints, begun, laid, swap, *near, *far)
    same, other = to_transposed(same, 0, 0), to_transposed(other, 0, 1)
    late = [along_y(block, dy) for dy, block in ((1, late_1), (2, late_2), (3, late_3))]
    joined = call(join_kernel, [VMEM] * 4, [four] * 2, [VMEM] * 2, [], 4, 10**7)(late_0, *late)
    joined = [to_transposed(block, 1, dx) for dx, block in enumerate(joined)]
    early = call(split_kernel, [VMEM] * 2, [two] * 3, [VMEM] * 3, [], 4, 10**7)(same, other)
    early = [along_y(block, dy) for dy, block in enumerate(early, 1)]
    return call(
        finish_kernel,
        [SMEM, SMEM, SMEM] + [VMEM] * 9,
        shape((8, 16, 8, LANES), F32),
        HBM,
        [
            pltpu.VMEM((2, 2, 64, 1024), F32),
            pltpu.VMEM((256, 1024), BF),
            pltpu.VMEM((8, 16, 8, LANES), F32),
            pltpu.SemaphoreType.DMA((8,)),
        ],
        12,
        10**9,
    )(ladder_tiles, cycle_tiles, partner, total, place_matrix(), same, other, *early, *joined)


def solution(mesh):
    placed = (
        P("pi", "pj", None, "vert"),
        P(None, "vert", None),
        P(),
        P("pj", None, None, "vert"),
        P(),
        P(),
    )
    return jax.shard_map(
        body, mesh=mesh, in_specs=placed, out_specs=P("pi", "pj", None, "vert"), check_vma=False
    )
```
